512 devices in a mesh: vol: 16 (over z_lo, y), img: 32 (over z_hi, x, core).
Axes of the slice: x: 4, y: 8, z: 8 (z_hi: 4, z_lo: 2; z = z_hi * 2 + z_lo), core: 2. Of those that a mesh axis runs over, the one named last changes fastest.
Arguments:
- volume: bfloat16 [256, 256, 256], P('vol', 'img'), may hold values from -6 to 6
- images: bfloat16 [16384, 256, 256], P('img', 'vol'), may hold values from -6 to 6
- bin_lists: int32 [32, 16], P('img'), may hold values from 0 to 63, all different within a row
- bin_planes: int32 [64], replicated, may hold values from 0 to 255
- bin_tilts: float32 [64], replicated, may hold values from -1 to 1
- defocus: float32 [32], replicated, may hold values from 20 to 80
- groups: int32 [16384], P('img'), may hold values from 0 to 31
- precision: float32 [16384], P('img'), may hold values from 1 to 40
Outputs:
- posteriors: float32 [16384, 16], P('img')
- numerator: float32 [256, 256, 256], P('vol', None, 'img')
The draws below stay inside these ranges and needn't reach their ends.
Inputs may be any that keep to these rules, and one draw needn't show every extreme that they name: `bin_lists`: each row names 16 different bins; every bin is named by some row.
All inputs are finite; a program needn't handle non-finite values.
Results may differ from the reference program's by a relative error of at most 0.02.
Values may be sent and summed in bfloat16 or wider, within the bound.
No kernel may reach another device: no remote copies, remote signals or barrier semaphores. Data moves between devices by JAX's collectives and lax.ppermute only.
A program may use at most 64 MiB of HBM per device.

```python
import math
import jax
import jax.numpy as jnp
import numpy as np
from jax import lax

Y = 256
X = 256
ZD = 16
ORI = 16
OB = 64
GROUPS = 32
IMG_DEV = 512
NZ = 256
IMAGES = 16384
BLOCKS = 32
N_VOL = 16


def draw_precision(key, part):
    key = jax.random.fold_in(key, 5)
    first_key = jax.random.fold_in(key, 0)
    values = 4.0 ** jax.random.uniform(first_key, (IMAGES,), jnp.float32)
    return values


def set_ends(values, own_key, low, largest):
    spot = [jax.random.randint(jax.random.fold_in(own_key, axis), (), 0, length) for axis, length in enumerate(values.shape)]
    longest = values.shape.index(max(values.shape))
    neighbour = spot[:longest] + [(spot[longest] + 1) % values.shape[longest]] + spot[longest + 1:]
    return values.at[tuple(spot)].set(low).at[tuple(neighbour)].set(largest)


def level_of(stream_key, dims, cuts, least, high):
    gain, own = 1.0, jax.random.fold_in(stream_key, 6)
    for position, parts in cuts:
        steps = jnp.exp(jax.random.uniform(jax.random.fold_in(own, position), (parts,), jnp.float32, least / len(cuts), high / len(cuts)))
        gain = gain * jnp.repeat(steps, dims[position] // parts).reshape([-1 if axis == position else 1 for axis in range(len(dims))])
    return gain


def cumulative_ranks(count, lean):
    portions = [(1 << 20) // math.isqrt(rank ** lean) + 1 for rank in range(1, count + 1)]
    scale = 1 + sum(portions) // (1 << 30)
    return np.cumsum(np.array([max(1, weight // scale) for weight in portions]))


def ranked_ids(stream_key, shape, count, skew):
    table = cumulative_ranks(count, skew)
    ticket = jax.random.randint(jax.random.fold_in(stream_key, 1), shape, 0, int(table[count - 1]))
    grade = jnp.searchsorted(jnp.asarray(table, jnp.int32), ticket, side="right")
    return jax.random.permutation(jax.random.fold_in(stream_key, 2), count)[grade].astype(jnp.int32)


def distinct(own_key, rows, amount, top, lift):
    ranking = jax.random.permutation(jax.random.fold_in(own_key, 1), amount)
    favour = ranking
    for power in range(3):
        favour = favour * favour // amount
    favour = favour * lift // amount
    tickets = jax.random.randint(jax.random.fold_in(own_key, 2), (rows, amount), 0, 4096) + favour
    sure = jax.random.permutation(jax.random.fold_in(own_key, 3), rows)[jnp.arange(amount) % rows]
    tickets = jnp.where(jnp.arange(rows)[:, None] == sure[None, :], 1 << 14, tickets)
    score = tickets * amount + jnp.arange(amount)
    return lax.top_k(score.astype(jnp.int32), top)[1].astype(jnp.int32)


def centred(rng, dims, deviation, bound, cuts=(), kind=jnp.bfloat16):
    values = jax.random.normal(rng, dims, jnp.float32) * deviation
    if len(cuts) > 0:
        values = level_of(rng, dims, cuts, -0.22, 0.18) * values
    return jnp.clip(values, min=-bound, max=bound).astype(kind)


def setup_inputs(seed: int = 0) -> dict:
    splits = jax.random.split(jax.random.key(seed), 9)
    return {
        "volume": centred(splits[0], (NZ, Y, X), 1.0, 6.0, ((0, 16), (1, 32))),
        "images": centred(splits[1], (IMAGES, Y, X), 1.0, 6.0, ((0, 32), (1, 16))),
        "bin_lists": distinct(splits[2], BLOCKS, OB, ORI, 4096),
        "bin_planes": set_ends(ranked_ids(splits[3], (OB,), NZ, 2), jax.random.fold_in(splits[3], 3), 0, NZ - 1).astype(jnp.int32),
        "bin_tilts": jnp.clip(jax.random.uniform(splits[4], (OB,), jnp.float32, -1.0, 1.0), -1.0, 1.0),
        "defocus": jnp.clip(jnp.exp(jax.random.uniform(splits[5], (GROUPS,), jnp.float32, math.log(20.0), math.log(80.0))), 20.0, 80.0),
        "groups": set_ends(jax.random.randint(splits[6], (IMAGES,), 0, GROUPS), jax.random.fold_in(splits[6], 1), 0, GROUPS - 1).astype(jnp.int32),
        "precision": draw_precision(jax.random.fold_in(splits[8], 71), 0),
    }


amplitude = 0.1
phase_part = math.sqrt(0.99)
epsilon = 1e-05

def section_weights(planes, tilt_vals, row_ids, plane_ids, height, reach_planes):
    centered = (row_ids.astype(jnp.float32) - (height - 1) * 0.5) * (2.0 / height)
    depth_pos = planes[:, None] + tilt_vals[:, None] * (reach_planes * centered)[None, :]
    distance = plane_ids.astype(jnp.float32)[None, None, :] - depth_pos[:, :, None]
    return jnp.maximum(0.0, 1.0 - jnp.abs(distance)).astype(jnp.bfloat16)

def ctf_table(defocus, row_ids, height, col_count):
    row_freq = (row_ids.astype(jnp.float32) - height // 2) * (2.0 / height)
    col_freq = (jnp.arange(col_count).astype(jnp.float32) - col_count // 2) * (2.0 / col_count)
    radius_sq = row_freq[:, None] ** 2 + col_freq[None, :] ** 2
    phase_shift = 0.5 * math.pi * defocus[:, None, None] * radius_sq[None, :, :]
    return -(phase_part * jnp.sin(phase_shift) + amplitude * jnp.cos(phase_shift))

def reference(volume, images, bin_lists, bin_planes, bin_tilts, defocus, groups, precision):
    ctf_rows = ctf_table(defocus, jnp.arange(Y), Y, X)
    square_ctf = ctf_rows * ctf_rows
    slab_data = volume.reshape(N_VOL, ZD, Y, X).astype(jnp.float32)
    row_ids = jnp.arange(Y)
    plane_ids = jnp.arange(NZ)

    def one_block(running, block_data):
        pictures, chosen, kind_ids, sharpness = block_data
        planes = bin_planes[chosen].astype(jnp.float32)
        tilt_vals = bin_tilts[chosen]
        kernel = section_weights(planes, tilt_vals, row_ids, plane_ids, Y, float(ZD)).astype(jnp.float32)
        slab_parts = jnp.einsum('oyvz,vzyx->voyx', kernel.reshape(ORI, Y, N_VOL, ZD), slab_data)
        slab_parts = lax.optimization_barrier(slab_parts.astype(jnp.bfloat16))
        templates = lax.optimization_barrier(jnp.sum(slab_parts.astype(jnp.float32), axis=0)).astype(jnp.bfloat16)
        templates = lax.optimization_barrier(templates).astype(jnp.float32)
        weighted = (pictures.astype(jnp.float32) * ctf_rows[kind_ids]).astype(jnp.bfloat16)
        weighted = lax.optimization_barrier(weighted).astype(jnp.float32)
        scores = jnp.einsum('nyx,oyx->no', weighted, templates)
        energy = jnp.einsum('gyx,oyx->go', square_ctf, templates * templates, precision=lax.Precision.HIGHEST)
        logits = sharpness[:, None] * scores / jnp.sqrt(energy[kind_ids] + epsilon)
        posterior = jax.nn.softmax(logits, axis=1)
        post_round = lax.optimization_barrier(posterior.astype(jnp.bfloat16)).astype(jnp.float32)
        summed_rows = jnp.einsum('no,nyx->oyx', post_round, weighted).astype(jnp.bfloat16)
        summed_rows = lax.optimization_barrier(summed_rows).astype(jnp.float32)
        backprojected = jnp.einsum('oyz,oyx->zyx', kernel, summed_rows).astype(jnp.bfloat16)
        backprojected = lax.optimization_barrier(backprojected)
        return (running + backprojected.astype(jnp.float32), posterior)
    initial = jnp.zeros((NZ, Y, X), jnp.float32)
    stacked = (images.reshape(BLOCKS, IMG_DEV, Y, X), bin_lists, groups.reshape(BLOCKS, IMG_DEV), precision.reshape(BLOCKS, IMG_DEV))
    numerator, posteriors = lax.scan(one_block, initial, stacked)
    return (posteriors.reshape(IMAGES, ORI), numerator)
```

```python
import functools
import math

import jax
import jax.numpy as jnp
from jax import lax
from jax.experimental import pallas as pl
from jax.experimental.pallas import tpu as pltpu
from jax.sharding import PartitionSpec as P

phase_offset = math.asin(0.1) / math.pi
epsilon = 1e-05
bf16 = jnp.bfloat16
f32 = jnp.float32
LANES = 128
VMEM = pl.BlockSpec(memory_space=pltpu.VMEM)
SMEM = pl.BlockSpec(memory_space=pltpu.SMEM)


def call(body, out_shape, in_specs, out_specs, scratch=(), grid=(), flops=0, nbytes=0, vmem=48):
    return pl.pallas_call(
        body,
        out_shape=out_shape,
        grid=grid,
        in_specs=in_specs,
        out_specs=out_specs,
        scratch_shapes=list(scratch),
        cost_estimate=pl.CostEstimate(flops=flops, bytes_accessed=nbytes, transcendentals=0),
        compiler_params=pltpu.CompilerParams(vmem_limit_bytes=vmem * 2**20),
    )


def dot(a, b, contract):
    return lax.dot_general(a, b, ((contract[0], contract[1]), ((), ())), preferred_element_type=f32)


def minus_sine_pi(turns):
    whole = jnp.floor(turns + 0.5)
    rest = turns - whole
    odd = whole - 2.0 * jnp.floor(whole * 0.5)
    x = rest * math.pi
    square = x * x
    total = -1.0 / 39916800.0
    for term in (1.0 / 362880.0, -1.0 / 5040.0, 1.0 / 120.0, -1.0 / 6.0, 1.0):
        total = total * square + term
    return total * x * (2.0 * odd - 1.0)


def swap_blocks(parts, stride):
    count = len(parts)
    lane = lax.broadcasted_iota(jnp.int32, parts[0].shape, parts[0].ndim - 1)
    bit = 1
    while bit < count:
        shift = stride * bit
        low = (lane & shift) == 0
        axis = parts[0].ndim - 1
        result = list(parts)
        for i in range(count):
            if i & bit:
                continue
            a, c = parts[i], parts[i | bit]
            result[i] = jnp.where(low, a, pltpu.roll(c, shift, axis))
            result[i | bit] = jnp.where(low, pltpu.roll(a, LANES - shift, axis), c)
        parts = result
        bit *= 2
    return parts


def weigh_body(block, rows, cols, group_total, first_row, defocus, groups, images, out, square, table, spread, square_spread):
    halves = cols // LANES

    @pl.when(pl.program_id(0) == 0)
    def _():
        row = (lax.broadcasted_iota(jnp.int32, (rows, cols), 0) + first_row[0]).astype(f32)
        col = lax.broadcasted_iota(jnp.int32, (rows, cols), 1).astype(f32)
        row_freq = (row - rows * 8.0) * (2.0 / (rows * 16.0))
        col_freq = (col - cols // 2) * (2.0 / cols)
        radius = 0.5 * (row_freq * row_freq + col_freq * col_freq)

        def one(g, _):
            value = minus_sine_pi(radius * defocus[g] + phase_offset)
            table[g] = value
            value = value * value
            for h in range(halves):
                square_spread[h, pl.ds(g, rows, stride=group_total), :] = value[:, h * LANES : (h + 1) * LANES]
            return 0

        lax.fori_loop(0, group_total, one, 0, unroll=4)
        for r in range(rows):
            for h in range(halves):
                value = square_spread[h, r * group_total : (r + 1) * group_total, :]
                high = value.astype(bf16)
                square[r, 0, :, h * LANES : (h + 1) * LANES] = high
                square[r, 1, :, h * LANES : (h + 1) * LANES] = (value - high.astype(f32)).astype(bf16)

    base = pl.program_id(0) * block

    def one(n, _):
        value = images[n].astype(f32) * table[groups[base + n]]
        for h in range(halves):
            spread[h, pl.ds(n, rows, stride=block), :] = value[:, h * LANES : (h + 1) * LANES]
        return 0

    lax.fori_loop(0, block, one, 0, unroll=8)
    for r in range(rows):
        for h in range(halves):
            out[r, :, h * LANES : (h + 1) * LANES] = spread[h, r * block : (r + 1) * block, :].astype(bf16)


def template_body(planes, bins, depth, received, out):
    sources = received.shape[0]
    total = sources * planes
    where = lax.broadcasted_iota(jnp.int32, (bins, total), 1).astype(f32)
    deep = jnp.concatenate([depth[...]] * (total // LANES), axis=1)
    weight = jnp.maximum(0.0, 1.0 - jnp.abs(where - deep)).astype(bf16)
    rows = received[:, :planes, :].reshape(total, LANES)
    chosen = received[:, planes:, :].reshape(-1, LANES)
    table = dot(weight, rows, ((1,), (0,))).astype(bf16)
    empty = jnp.zeros_like(table)
    listed = chosen.shape[0] // sources
    low = dot(chosen, jnp.concatenate([table, empty], axis=0), ((1,), (0,))).astype(bf16)
    high = dot(chosen, jnp.concatenate([empty, table], axis=0), ((1,), (0,))).astype(bf16)
    out[:sources] = low.reshape(sources, listed, LANES)
    out[sources:] = high.reshape(sources, listed, LANES)


def score_body(templates, weighted, square, out, scores, energy):
    step = pl.program_id(0)
    rows = weighted.shape[0]
    total = None
    power = None
    for r in range(rows):
        piece = jnp.concatenate([templates[2 * r], templates[2 * r + 1]], axis=1)
        part = dot(piece, weighted[r], ((1,), (1,)))
        total = part if total is None else total + part
        wide = piece.astype(f32)
        wide = wide * wide
        high = wide.astype(bf16)
        low = (wide - high.astype(f32)).astype(bf16)
        left = jnp.concatenate([high, high, low], axis=1)
        right = jnp.concatenate([square[r, 0], square[r, 1], square[r, 0]], axis=1)
        part = dot(left, right, ((1,), (1,)))
        power = part if power is None else power + part
    group_total = power.shape[1]

    @pl.when(step == 0)
    def _():
        scores[...] = total
        energy[...] = jnp.zeros_like(energy)
        energy[:, :group_total] = power

    @pl.when(step > 0)
    def _():
        scores[...] += total
        energy[:, :group_total] += power

    @pl.when(step == pl.num_programs(0) - 1)
    def _():
        chunks = scores.shape[1] // LANES
        listed = scores.shape[0]
        values = [scores[:, c * LANES : (c + 1) * LANES] for c in range(chunks)]
        tail = energy[: listed // 2] + pltpu.roll(energy[listed // 2 :], group_total, 1)
        for k in range(out.shape[0]):
            for c in range(chunks):
                out[k, c * listed : (c + 1) * listed, :] = values[c]
            out[k, chunks * listed :, :] = tail


def posterior_body(group_total, partial, groups, sharpness, weighted, posteriors, out, rounded):
    step = pl.program_id(0)
    listed = posteriors.shape[0]
    images = posteriors.shape[1]

    @pl.when(step == 0)
    def _():
        summed = partial[0]
        for k in range(1, partial.shape[0]):
            summed = summed + partial[k]
        chunks = images // LANES
        scores = jnp.concatenate([summed[c * listed : (c + 1) * listed] for c in range(chunks)], axis=1)
        scale = 1.0 / jnp.sqrt(summed[chunks * listed :] + epsilon)
        scale = jnp.concatenate([scale, pltpu.roll(scale, LANES - group_total, 1)], axis=0)
        member = lax.broadcasted_iota(jnp.int32, (LANES, images), 0) == groups[...]
        member = member.astype(f32)
        picked = lax.dot_general(
            scale, member, (((1,), (0,)), ((), ())), precision=lax.Precision.HIGHEST, preferred_element_type=f32
        )
        logits = sharpness[...] * scores * picked
        logits = jnp.exp(logits - jnp.max(logits, axis=0, keepdims=True))
        result = logits / jnp.sum(logits, axis=0, keepdims=True)
        posteriors[...] = result
        rounded[...] = result.astype(bf16)

    rows = weighted.shape[0]
    for r in range(rows):
        part = dot(rounded[...], weighted[r], ((1,), (0,)))
        out[r] = part


def spread_body(summed, out):
    rows, listed, cols = summed.shape
    for o in range(0, listed, 8):
        for h in range(cols // LANES):
            parts = [summed[r, o : o + 8, h * LANES : (h + 1) * LANES] for r in range(rows)]
            parts = swap_blocks(parts, LANES // rows)
            for j in range(rows):
                out[h * rows + j, o : o + 8, :] = parts[j].astype(bf16)


def project_body(planes, bins, reach, centre, tilt, chosen, arrived, out):
    sources = chosen.shape[0]
    half = sources * (chosen.shape[1] - planes)
    picker = chosen[:, planes:, :].reshape(half, LANES)
    both = arrived[...].reshape(2 * half, LANES)
    low = dot(both[:half], picker, ((0,), (0,)))
    high = dot(both[half:], picker, ((0,), (0,)))
    lane = lax.broadcasted_iota(jnp.int32, low.shape, 1)
    by_bin = jnp.where(lane < bins, low, high)
    rows = reach.shape[0]
    width = LANES // rows
    parts = []
    lane = lax.broadcasted_iota(jnp.int32, (bins, LANES), 1)
    for r in range(rows):
        deep = centre[...] + tilt[...] * reach[r]
        weights = []
        for h in range(2):
            where = ((lane % 16) * planes + h * 8 + lane // 16).astype(f32)
            weights.append(jnp.maximum(0.0, 1.0 - jnp.abs(where - deep)).astype(bf16))
        weight = jnp.concatenate(weights, axis=1)
        weight = jnp.concatenate([weight, weight], axis=0)
        parts.append(dot(by_bin[r * width : (r + 1) * width].astype(bf16), weight, ((1,), (0,))))
    first = swap_blocks([part[:, :LANES] for part in parts], 1)
    second = swap_blocks([part[:, LANES:] for part in parts], 1)
    for j in range(rows):
        out[j] = jnp.concatenate([first[j], second[j]], axis=0).astype(bf16)


def final_body(arrived, out):
    bands = arrived.shape[0]
    wide = arrived[...].astype(f32)
    for zh in range(2):
        for vh in range(bands // 8):
            parts = [wide[vh * 8 + k, zh * 8 : (zh + 1) * 8, :] for k in range(8)]
            parts = swap_blocks(parts, LANES // 8)
            for zl in range(8):
                out[zh * 8 + zl, :, vh * LANES : (vh + 1) * LANES] = parts[zl]


def per_device(volume, images, bin_lists, bin_planes, bin_tilts, defocus, groups, precision):
    bands = lax.axis_size("vol")
    blocks = lax.axis_size("img")
    half_group = blocks // 2
    planes, strip, cols = volume.shape
    image_count, rows, _ = images.shape
    height = rows * bands
    bins = bin_planes.shape[0]
    listed = bin_lists.shape[1]
    group_total = defocus.shape[0]
    lane_halves = cols // LANES
    vol_index = lax.axis_index("vol")
    img_index = lax.axis_index("img")
    halves = [list(range(half_group)), list(range(half_group, blocks))]

    sent = volume.reshape(planes, strip, lane_halves, LANES).transpose(1, 2, 0, 3)
    sent = sent.reshape(strip * lane_halves, planes, LANES)
    route = [
        (v * blocks + i, (i // 2) * blocks + (i % 2) * half_group + v)
        for v in range(bands)
        for i in range(blocks)
    ]
    moved = lax.ppermute(sent, ("vol", "img"), route)

    other = lax.ppermute(bin_lists, "img", [(i, (i + half_group) % blocks) for i in range(blocks)])
    upper = img_index >= half_group
    low_list = jnp.where(upper, other[0], bin_lists[0])
    high_list = jnp.where(upper, bin_lists[0], other[0])
    lane_ids = jnp.arange(2 * bins)[None, :]
    chosen = (lane_ids == low_list[:, None]) | (lane_ids == high_list[:, None] + bins)
    chosen = chosen.astype(bf16)

    first_row = vol_index * rows
    own_row = first_row + img_index // 2

    def reach_of(ids):
        return float(planes) * ((ids.astype(f32) - (height - 1) * 0.5) * (2.0 / height))

    centre = jnp.broadcast_to(bin_planes.astype(f32)[:, None], (bins, LANES))
    tilt = jnp.broadcast_to(bin_tilts[:, None], (bins, LANES))
    depth = centre + tilt * reach_of(own_row)
    reach = reach_of(first_row + jnp.arange(rows))

    block = 64
    weighted, square = call(
        functools.partial(weigh_body, block, rows, cols, group_total),
        (
            jax.ShapeDtypeStruct((rows, image_count, cols), bf16),
            jax.ShapeDtypeStruct((rows, 2, group_total, cols), bf16),
        ),
        [SMEM, SMEM, SMEM, pl.BlockSpec((block, rows, cols), lambda i: (i, 0, 0))],
        (
            pl.BlockSpec((rows, block, cols), lambda i: (0, i, 0)),
            pl.BlockSpec((rows, 2, group_total, cols), lambda i: (0, 0, 0, 0)),
        ),
        scratch=(
            pltpu.VMEM((group_total, rows, cols), f32),
            pltpu.VMEM((lane_halves, rows * block, LANES), f32),
            pltpu.VMEM((lane_halves, rows * group_total, LANES), f32),
        ),
        grid=(image_count // block,),
        flops=40 * image_count * rows * cols,
        nbytes=4 * image_count * rows * cols,
    )(first_row.reshape(1), defocus, groups, images)

    packed = jnp.concatenate(
        [moved, jnp.broadcast_to(chosen[None], (half_group,) + chosen.shape)], axis=1
    )
    gathered = lax.all_to_all(packed, "img", 0, 0, tiled=True, axis_index_groups=halves)
    pieces = call(
        functools.partial(template_body, planes, bins),
        jax.ShapeDtypeStruct((blocks, listed, LANES), bf16),
        [VMEM, VMEM],
        VMEM,
    )(depth, gathered)
    templates = lax.all_to_all(pieces, "img", 0, 0, tiled=True)

    step_rows = 4
    payload_rows = listed * (image_count // LANES) + listed // 2
    partial = call(
        score_body,
        jax.ShapeDtypeStruct((bands, payload_rows, LANES), f32),
        [
            pl.BlockSpec((step_rows * lane_halves, listed, LANES), lambda i: (i, 0, 0)),
            pl.BlockSpec((step_rows, image_count, cols), lambda i: (i, 0, 0)),
            pl.BlockSpec((step_rows, 2, group_total, cols), lambda i: (i, 0, 0, 0)),
        ],
        pl.BlockSpec((bands, payload_rows, LANES), lambda i: (0, 0, 0)),
        scratch=(pltpu.VMEM((listed, image_count), f32), pltpu.VMEM((listed, LANES), f32)),
        grid=(rows // step_rows,),
    )(templates, weighted, square)
    partial = lax.all_to_all(partial, "vol", 0, 0, tiled=True)

    posteriors, summed = call(
        functools.partial(posterior_body, group_total),
        (
            jax.ShapeDtypeStruct((listed, image_count), f32),
            jax.ShapeDtypeStruct((rows, listed, cols), f32),
        ),
        [
            VMEM_BLOCK((bands, payload_rows, LANES)),
            VMEM_BLOCK((1, image_count)),
            VMEM_BLOCK((1, image_count)),
            pl.BlockSpec((step_rows, image_count, cols), lambda i: (i, 0, 0)),
        ],
        (
            VMEM_BLOCK((listed, image_count)),
            pl.BlockSpec((step_rows, listed, cols), lambda i: (i, 0, 0)),
        ),
        scratch=(pltpu.VMEM((listed, image_count), bf16),),
        grid=(rows // step_rows,),
    )(partial, groups.reshape(1, image_count), precision.reshape(1, image_count), weighted)
    spread = call(
        spread_body,
        jax.ShapeDtypeStruct((blocks, listed, LANES), bf16),
        [VMEM],
        VMEM,
    )(summed)
    arrived = lax.all_to_all(spread, "img", 0, 0, tiled=True)

    projected = call(
        functools.partial(project_body, planes, bins),
        jax.ShapeDtypeStruct((bands, planes, LANES), bf16),
        [SMEM, VMEM, VMEM, VMEM, VMEM],
        VMEM,
    )(reach, centre, tilt, gathered, arrived)
    slabs = lax.all_to_all(projected, "vol", 0, 0, tiled=True)
    numerator = call(
        final_body,
        jax.ShapeDtypeStruct((planes, cols // blocks, height), f32),
        [VMEM],
        VMEM,
    )(slabs)
    return (posteriors.T, numerator.transpose(0, 2, 1))


def VMEM_BLOCK(shape):
    return pl.BlockSpec(shape, lambda i: (0,) * len(shape))


def solution(mesh):
    placed = (
        P("vol", "img", None),
        P("img", "vol", None),
        P("img", None),
        P(),
        P(),
        P(),
        P("img"),
        P("img"),
    )
    return jax.shard_map(
        per_device,
        mesh=mesh,
        in_specs=placed,
        out_specs=(P("img", None), P("vol", None, "img")),
        check_vma=False,
    )
```

```python
import functools
import math

import jax
import jax.numpy as jnp
from jax import lax
from jax.experimental import pallas as pl
from jax.experimental.pallas import tpu as pltpu
from jax.sharding import PartitionSpec as P

phase_offset = math.asin(0.1) / math.pi
epsilon = 1e-05
bf16 = jnp.bfloat16
f32 = jnp.float32
LANES = 128
VMEM = pl.BlockSpec(memory_space=pltpu.VMEM)
SMEM = pl.BlockSpec(memory_space=pltpu.SMEM)


def call(body, out_shape, in_specs, out_specs, scratch=(), grid=(), flops=0, nbytes=0, vmem=16):
    return pl.pallas_call(
        body,
        out_shape=out_shape,
        grid=grid,
        in_specs=in_specs,
        out_specs=out_specs,
        scratch_shapes=list(scratch),
        cost_estimate=pl.CostEstimate(flops=flops, bytes_accessed=nbytes, transcendentals=0),
        compiler_params=pltpu.CompilerParams(vmem_limit_bytes=vmem * 2**20),
    )


def in_hbm(*arrays):
    return [pltpu.with_memory_space_constraint(array, pltpu.HBM) for array in arrays]


def dot(a, b, contract):
    return lax.dot_general(a, b, ((contract[0], contract[1]), ((), ())), preferred_element_type=f32)


def minus_sine_pi(turns):
    whole = jnp.floor(turns + 0.5)
    rest = turns - whole
    odd = whole - 2.0 * jnp.floor(whole * 0.5)
    x = rest * math.pi
    square = x * x
    total = -1.0 / 39916800.0
    for term in (1.0 / 362880.0, -1.0 / 5040.0, 1.0 / 120.0, -1.0 / 6.0, 1.0):
        total = total * square + term
    return total * x * (2.0 * odd - 1.0)


def swap_blocks(parts, stride):
    count = len(parts)
    lane = lax.broadcasted_iota(jnp.int32, parts[0].shape, parts[0].ndim - 1)
    bit = 1
    while bit < count:
        shift = stride * bit
        low = (lane & shift) == 0
        axis = parts[0].ndim - 1
        result = list(parts)
        for i in range(count):
            if i & bit:
                continue
            a, c = parts[i], parts[i | bit]
            result[i] = jnp.where(low, a, pltpu.roll(c, shift, axis))
            result[i | bit] = jnp.where(low, pltpu.roll(a, LANES - shift, axis), c)
        parts = result
        bit *= 2
    return parts


def row_of(rows):
    return lax.axis_index("vol") * rows


def reach_of(row, planes, height):
    return float(planes) * ((row.astype(f32) - (height - 1) * 0.5) * (2.0 / height))


def one_hot(mask):
    return mask.astype(f32).astype(bf16)


def part_body(lists, volume, out):
    planes, strip, cols = volume.shape
    size = planes * strip
    here = lax.broadcasted_iota(jnp.int32, (size, size), 0)
    there = lax.broadcasted_iota(jnp.int32, (size, size), 1)
    mixer = one_hot((here % planes) * strip + here // planes == there)
    mixed = dot(mixer, volume[...].astype(f32).reshape(size, cols).astype(bf16), ((1,), (0,)))
    place = lax.broadcasted_iota(jnp.int32, (planes, LANES), 0)
    lane = lax.broadcasted_iota(jnp.int32, (planes, LANES), 1)
    half = LANES // 2
    hit = (place == 0) & (lane == lists[0] + half)
    for o in range(1, planes):
        hit = hit | ((place == o) & (lane == lists[o] + half))
    listed = hit.astype(f32)
    for h in range(cols // LANES):
        parts = [mixed[r * planes : (r + 1) * planes, h * LANES : (h + 1) * LANES] for r in range(strip)]
        parts = swap_blocks(parts, half // strip)
        for j in range(strip):
            piece = parts[j]
            out[h * 2 * strip + j] = jnp.where(lane < half, piece, listed).astype(bf16)
            out[h * 2 * strip + strip + j] = jnp.where(lane < half, pltpu.roll(piece, half, 1), listed).astype(bf16)


def weigh_body(block, first_row, defocus, groups, bin_planes, bin_tilts, images, out, square, centre, tilt, table, mixer, held, power):
    _, rows, cols = images.shape
    group_total = table.shape[0]

    @pl.when(pl.program_id(0) == 0)
    def _():
        row = (lax.broadcasted_iota(jnp.int32, (rows, cols), 0) + first_row[0]).astype(f32)
        col = lax.broadcasted_iota(jnp.int32, (rows, cols), 1).astype(f32)
        row_freq = (row - cols // 2) * (2.0 / cols)
        col_freq = (col - cols // 2) * (2.0 / cols)
        radius = 0.5 * (row_freq * row_freq + col_freq * col_freq)

        def one(g, _):
            value = minus_sine_pi(radius * defocus[g] + phase_offset)
            table[g] = value
            value = value * value
            high = value.astype(bf16)
            power[0, g] = high
            power[1, g] = (value - high.astype(f32)).astype(bf16)
            return 0

        lax.fori_loop(0, group_total, one, 0, unroll=4)
        size = mixer.shape[0]
        here = lax.broadcasted_iota(jnp.int32, (size, size), 0)
        there = lax.broadcasted_iota(jnp.int32, (size, size), 1)
        mixer[...] = one_hot((here % rows) * rows + here // rows == there)
        for part in range(2):
            for g in range(0, group_total, rows):
                mixed = dot(mixer[...], power[part, g : g + rows].reshape(rows * rows, cols), ((1,), (0,)))
                square[:, part, g : g + rows, :] = mixed.astype(bf16).reshape(rows, rows, cols)
        for q in range(centre.shape[0]):
            centre[q : q + 1, :] = jnp.full((1, LANES), bin_planes[q].astype(f32))
            tilt[q : q + 1, :] = jnp.full((1, LANES), bin_tilts[q])

    base = pl.program_id(0) * block

    def some(k, _):
        for m in range(rows):
            n = k * rows + m
            held[m] = (images[n].astype(f32) * table[groups[base + n]]).astype(bf16)
        mixed = dot(mixer[...], held[...].reshape(rows * rows, cols), ((1,), (0,)))
        out[:, pl.ds(k * rows, rows), :] = mixed.astype(bf16).reshape(rows, rows, cols)
        return 0

    lax.fori_loop(0, block // rows, some, 0, unroll=True)


def band_body(received, after, out):
    lane = lax.broadcasted_iota(jnp.int32, received.shape[1:], 1)
    half = LANES // 2
    for w in range(out.shape[0]):
        first = received[2 * w].astype(f32)
        second = pltpu.roll(received[2 * w + 1].astype(f32), half, 1)
        out[w] = jnp.where(lane < half, first, second).astype(bf16)


def template_body(rows, height, first_row, centre, tilt, received, planes, out):
    bands, slab, _ = planes.shape
    bins = centre.shape[0]
    total = bands * slab
    where = lax.broadcasted_iota(jnp.int32, (bins, total), 1).astype(f32)
    weights = []
    for r in range(rows):
        deep = centre[...] + tilt[...] * reach_of(first_row[0] + r, slab, height)
        deep = jnp.concatenate([deep] * (total // LANES), axis=1)
        weights.append(jnp.maximum(0.0, 1.0 - jnp.abs(where - deep)).astype(bf16))
    every = dot(jnp.concatenate(weights, axis=0), planes[...].reshape(total, LANES), ((1,), (0,)))
    lane = lax.broadcasted_iota(jnp.int32, (bins, LANES), 1)
    table = every[:bins]
    for r in range(1, rows):
        table = jnp.where(lane // (LANES // rows) == r, every[r * bins : (r + 1) * bins], table)
    table = jnp.concatenate([jnp.zeros((LANES - bins, LANES), bf16), table.astype(bf16)], axis=0)
    chosen = received[...].reshape(-1, LANES)
    out[...] = dot(chosen, table, ((1,), (0,))).astype(bf16).reshape(out.shape)


top = 32767.0


def level_code(largest):
    code = jnp.floor(256.0 * jnp.log2(jnp.maximum(largest, 1e-30))) + 2.0
    return code, jnp.exp2(code * (-1.0 / 256.0))


def level_of(code):
    return jnp.exp2(code * (1.0 / 256.0))


def diagonal(count):
    shape = (count, LANES)
    return lax.broadcasted_iota(jnp.int32, shape, 0) == lax.broadcasted_iota(jnp.int32, shape, 1)


def score_body(templates, weighted, square, out, extra):
    rows, images, cols = weighted.shape
    group_total = square.shape[0]
    listed = templates.shape[1]
    total = None
    power = None
    halves = []
    for h in range(cols // LANES):
        parts = [templates[h * rows + j].astype(f32) for j in range(rows)]
        halves.append(swap_blocks(parts, LANES // rows))
    for r in range(rows):
        piece = jnp.concatenate([half[r] for half in halves], axis=1).astype(bf16)
        part = dot(piece, weighted[r], ((1,), (1,)))
        total = part if total is None else total + part
        wide = piece.astype(f32)
        wide = wide * wide
        high = wide.astype(bf16)
        low = (wide - high.astype(f32)).astype(bf16)
        left = jnp.concatenate([high, high, low], axis=1)
        right = jnp.concatenate([square[r, 0], square[r, 1], square[r, 0]], axis=1)
        part = dot(left, right, ((1,), (1,)))
        power = part if power is None else power + part
    group_total = power.shape[1]
    extra[...] = jnp.zeros_like(extra)
    extra[:, :group_total] = power
    power = jnp.maximum(extra[...], 0.0)
    row_code, row_scale = level_code(jnp.max(jnp.abs(total), axis=1, keepdims=True))
    total = total * row_scale
    image_code, image_scale = level_code(jnp.max(jnp.abs(total), axis=0, keepdims=True))
    total = jnp.clip(jnp.floor(total * image_scale * top + 0.5), -top, top)
    power_code, power_scale = level_code(jnp.max(power, axis=1, keepdims=True))
    power = jnp.minimum(power * power_scale, 1.0) * top
    high = jnp.floor(power)
    low = jnp.floor((power - high) * top + 0.5)
    half = listed // 2
    extra[:half] = (
        high[:half]
        + pltpu.roll(high[half:], group_total, 1)
        + pltpu.roll(low[:half], 2 * group_total, 1)
        + pltpu.roll(low[half:], 3 * group_total, 1)
    )
    chunks = images // LANES
    for c in range(chunks):
        extra[half + c : half + c + 1, :] = image_code[:, c * LANES : (c + 1) * LANES]
    square_mask = diagonal(listed)
    for place, code in ((half + chunks, row_code), (half + chunks + 1, power_code)):
        extra[place : place + 1, :] = jnp.sum(jnp.where(square_mask, code, 0.0), axis=0, keepdims=True)
    extra[half + chunks + 2 :, :] = jnp.zeros((listed - half - chunks - 2, LANES), f32)
    pieces = [total[:, c * LANES : (c + 1) * LANES] for c in range(chunks)] + [extra[...]]
    pieces = [piece.astype(jnp.int32).astype(jnp.int16) for piece in pieces]
    for k in range(out.shape[0]):
        for c, piece in enumerate(pieces):
            out[k, c * listed : (c + 1) * listed, :] = piece


def posterior_body(group_total, partial, groups, sharpness, weighted, posteriors, out):
    listed, images = posteriors.shape
    rows, _, cols = weighted.shape
    chunks = images // LANES
    half = listed // 2
    square_mask = diagonal(listed)
    lane = lax.broadcasted_iota(jnp.int32, (half, LANES), 1)
    scores = None
    power = None
    for k in range(partial.shape[0]):
        value = partial[k].astype(jnp.int32).astype(f32)
        extra = value[chunks * listed :]
        row_level, power_level = (
            level_of(jnp.sum(jnp.where(square_mask, extra[place : place + 1], 0.0), axis=1, keepdims=True)) / top
            for place in (half + chunks, half + chunks + 1)
        )
        image_level = [level_of(extra[half + c : half + c + 1]) for c in range(chunks)]
        part = [value[c * listed : (c + 1) * listed] * row_level * image_level[c] for c in range(chunks)]
        scores = part if scores is None else [a + b for a, b in zip(scores, part)]
        part = extra[:half] + pltpu.roll(extra[:half], LANES - 2 * group_total, 1) * (1.0 / top)
        part = part * jnp.where(lane < group_total, power_level[:half], power_level[half:])
        power = part if power is None else power + part
    scores = jnp.concatenate(scores, axis=1)
    power = jnp.where(lane < 2 * group_total, power, 0.0)
    scale = 1.0 / jnp.sqrt(power + epsilon)
    scale = jnp.concatenate([scale, pltpu.roll(scale, LANES - group_total, 1)], axis=0)
    member = lax.broadcasted_iota(jnp.int32, (LANES, images), 0) == groups[...]
    member = member.astype(f32)
    picked = lax.dot_general(
        scale, member, (((1,), (0,)), ((), ())), precision=lax.Precision.HIGHEST, preferred_element_type=f32
    )
    logits = sharpness[...] * scores * picked
    logits = jnp.exp(logits - jnp.max(logits, axis=0, keepdims=True))
    result = logits / jnp.sum(logits, axis=0, keepdims=True)
    posteriors[...] = result
    rounded = result.astype(bf16)
    totals = [dot(rounded, weighted[r], ((1,), (0,))) for r in range(rows)]
    for h in range(cols // LANES):
        parts = [total[:, h * LANES : (h + 1) * LANES] for total in totals]
        parts = swap_blocks(parts, LANES // rows)
        for j in range(rows):
            out[h * rows + j] = parts[j].astype(bf16)


def project_body(rows, height, first_row, centre, tilt, received, arrived, out):
    bands, planes, _ = out.shape
    bins = centre.shape[0]
    pairs = arrived.shape[0] * arrived.shape[1]
    by_bin = dot(arrived[...].reshape(pairs, LANES), received[...].reshape(pairs, LANES), ((0,), (0,)))
    width = LANES // rows
    lane = lax.broadcasted_iota(jnp.int32, (bins, LANES), 1)
    empty = jnp.zeros((LANES - bins, 2 * LANES), bf16)
    parts = []
    for r in range(rows):
        deep = centre[...] + tilt[...] * reach_of(first_row[0] + r, planes, height)
        weights = []
        for h in range(2):
            where = ((lane % bands) * planes + h * (planes // 2) + lane // bands).astype(f32)
            weights.append(jnp.maximum(0.0, 1.0 - jnp.abs(where - deep)).astype(bf16))
        weight = jnp.concatenate([empty, jnp.concatenate(weights, axis=1)], axis=0)
        parts.append(dot(by_bin[r * width : (r + 1) * width].astype(bf16), weight, ((1,), (0,))))
    first = swap_blocks([part[:, :LANES] for part in parts], 1)
    second = swap_blocks([part[:, LANES:] for part in parts], 1)
    for j in range(bands):
        out[j] = jnp.concatenate([first[j], second[j]], axis=0).astype(bf16)


def final_body(arrived, out):
    bands = arrived.shape[0]
    wide = arrived[...].astype(f32)
    for zh in range(2):
        for vh in range(bands // 8):
            parts = [wide[vh * 8 + k, zh * 8 : (zh + 1) * 8, :] for k in range(8)]
            parts = swap_blocks(parts, LANES // 8)
            for zl in range(8):
                out[zh * 8 + zl, :, vh * LANES : (vh + 1) * LANES] = parts[zl]


def per_device(volume, images, bin_lists, bin_planes, bin_tilts, defocus, groups, precision):
    bands = lax.axis_size("vol")
    blocks = lax.axis_size("img")
    planes, strip, cols = volume.shape
    image_count, rows, _ = images.shape
    height = rows * bands
    bins = bin_planes.shape[0]
    listed = bin_lists.shape[1]
    group_total = defocus.shape[0]
    first_row = row_of(rows).reshape(1)

    sent = call(
        part_body,
        pltpu.HBM((blocks, planes, LANES), bf16),
        [SMEM, VMEM],
        VMEM,
    )(*in_hbm(bin_lists[0], volume))
    received = lax.all_to_all(sent, "img", 0, 0, tiled=True)

    block = 256
    weighted, square, centre, tilt = call(
        functools.partial(weigh_body, block),
        (
            pltpu.HBM((rows, image_count, cols), bf16),
            jax.ShapeDtypeStruct((rows, 2, group_total, cols), bf16),
            jax.ShapeDtypeStruct((bins, LANES), f32),
            jax.ShapeDtypeStruct((bins, LANES), f32),
        ),
        [SMEM] * 5 + [pl.BlockSpec((block, rows, cols), lambda i: (i, 0, 0))],
        (
            pl.BlockSpec((rows, block, cols), lambda i: (0, i, 0)),
            pl.BlockSpec((rows, 2, group_total, cols), lambda i: (0, 0, 0, 0)),
            pl.BlockSpec((bins, LANES), lambda i: (0, 0)),
            pl.BlockSpec((bins, LANES), lambda i: (0, 0)),
        ),
        scratch=(
            pltpu.VMEM((group_total, rows, cols), f32),
            pltpu.VMEM((rows * rows, rows * rows), bf16),
            pltpu.VMEM((rows, rows, cols), bf16),
            pltpu.VMEM((2, group_total, rows, cols), bf16),
        ),
        grid=(image_count // block,),
        flops=40 * image_count * rows * cols,
        nbytes=4 * image_count * rows * cols,
    )(first_row, *in_hbm(defocus, groups, bin_planes, bin_tilts, images))

    joined = call(
        band_body,
        jax.ShapeDtypeStruct((bands, planes, LANES), bf16),
        [VMEM, VMEM],
        VMEM,
    )(received, centre)
    stack = lax.all_to_all(joined, "vol", 0, 0, tiled=True)
    pieces = call(
        functools.partial(template_body, rows, height),
        jax.ShapeDtypeStruct((blocks, listed, LANES), bf16),
        [SMEM, VMEM, VMEM, VMEM, VMEM],
        VMEM,
    )(first_row, centre, tilt, received, stack)
    templates = lax.all_to_all(pieces, "img", 0, 0, tiled=True)

    payload_rows = listed * (image_count // LANES + 1)
    partial = call(
        score_body,
        jax.ShapeDtypeStruct((bands, payload_rows, LANES), jnp.int16),
        [VMEM, VMEM, VMEM],
        VMEM,
        scratch=(pltpu.VMEM((listed, LANES), f32),),
    )(templates, weighted, square)
    partial = lax.all_to_all(partial, "vol", 0, 0, tiled=True)

    posteriors, spread = call(
        functools.partial(posterior_body, group_total),
        (
            jax.ShapeDtypeStruct((listed, image_count), f32),
            jax.ShapeDtypeStruct((blocks, listed, LANES), bf16),
        ),
        [VMEM, VMEM, VMEM, VMEM],
        (VMEM, VMEM),
    )(partial, groups.reshape(1, image_count), precision.reshape(1, image_count), weighted)
    arrived = lax.all_to_all(spread, "img", 0, 0, tiled=True)

    projected = call(
        functools.partial(project_body, rows, height),
        jax.ShapeDtypeStruct((bands, planes, LANES), bf16),
        [SMEM, VMEM, VMEM, VMEM, VMEM],
        VMEM,
    )(first_row, centre, tilt, received, arrived)
    slabs = lax.all_to_all(projected, "vol", 0, 0, tiled=True)
    numerator = call(
        final_body,
        jax.ShapeDtypeStruct((planes, cols // blocks, height), f32),
        [VMEM],
        VMEM,
    )(slabs)
    return (posteriors.T, numerator.transpose(0, 2, 1))


def solution(mesh):
    placed = (
        P("vol", "img", None),
        P("img", "vol", None),
        P("img", None),
        P(),
        P(),
        P(),
        P("img"),
        P("img"),
    )
    return jax.shard_map(
        per_device,
        mesh=mesh,
        in_specs=placed,
        out_specs=(P("img", None), P("vol", None, "img")),
        check_vma=False,
    )
```

```python
import functools
import math

import jax
import jax.numpy as jnp
from jax import lax
from jax.experimental import pallas as pl
from jax.experimental.pallas import tpu as pltpu
from jax.sharding import PartitionSpec as P

phase_offset = math.asin(0.1) / math.pi
epsilon = 1e-05
bf16 = jnp.bfloat16
f32 = jnp.float32
LANES = 128
VMEM = pl.BlockSpec(memory_space=pltpu.VMEM)
SMEM = pl.BlockSpec(memory_space=pltpu.SMEM)


def call(body, out_shape, in_specs, out_specs, scratch=(), grid=(), flops=0, nbytes=0, vmem=16):
    return pl.pallas_call(
        body,
        out_shape=out_shape,
        grid=grid,
        in_specs=in_specs,
        out_specs=out_specs,
        scratch_shapes=list(scratch),
        cost_estimate=pl.CostEstimate(flops=flops, bytes_accessed=nbytes, transcendentals=0),
        compiler_params=pltpu.CompilerParams(vmem_limit_bytes=vmem * 2**20),
    )


def in_hbm(*arrays):
    return [pltpu.with_memory_space_constraint(array, pltpu.HBM) for array in arrays]


def dot(a, b, contract):
    return lax.dot_general(a, b, ((contract[0], contract[1]), ((), ())), preferred_element_type=f32)


def minus_sine_pi(turns):
    whole = jnp.floor(turns + 0.5)
    rest = turns - whole
    odd = whole - 2.0 * jnp.floor(whole * 0.5)
    x = rest * math.pi
    square = x * x
    total = -1.0 / 39916800.0
    for term in (1.0 / 362880.0, -1.0 / 5040.0, 1.0 / 120.0, -1.0 / 6.0, 1.0):
        total = total * square + term
    return total * x * (2.0 * odd - 1.0)


def swap_blocks(parts, stride):
    count = len(parts)
    lane = lax.broadcasted_iota(jnp.int32, parts[0].shape, parts[0].ndim - 1)
    bit = 1
    while bit < count:
        shift = stride * bit
        low = (lane & shift) == 0
        axis = parts[0].ndim - 1
        result = list(parts)
        for i in range(count):
            if i & bit:
                continue
            a, c = parts[i], parts[i | bit]
            result[i] = jnp.where(low, a, pltpu.roll(c, shift, axis))
            result[i | bit] = jnp.where(low, pltpu.roll(a, LANES - shift, axis), c)
        parts = result
        bit *= 2
    return parts


def row_of(rows):
    return lax.axis_index("vol") * rows


def reach_of(row, planes, height):
    return float(planes) * ((row.astype(f32) - (height - 1) * 0.5) * (2.0 / height))


def one_hot(mask):
    return mask.astype(f32).astype(bf16)


def part_body(lists, volume, out):
    planes, strip, cols = volume.shape
    size = planes * strip
    here = lax.broadcasted_iota(jnp.int32, (size, size), 0)
    there = lax.broadcasted_iota(jnp.int32, (size, size), 1)
    mixer = one_hot((here % planes) * strip + here // planes == there)
    mixed = dot(mixer, volume[...].astype(f32).reshape(size, cols).astype(bf16), ((1,), (0,)))
    lane = lax.broadcasted_iota(jnp.int32, (planes, LANES), 1)
    half = LANES // 2
    ids = jnp.concatenate([lists[...], jnp.zeros((1, LANES - planes), jnp.int32)], axis=1)
    ids = jnp.sum(jnp.where(diagonal(planes), ids, 0), axis=1, keepdims=True)
    listed = (lane == ids + half).astype(f32)
    place = 0
    for r in range(strip):
        for h in range(cols // LANES):
            piece = mixed[r * planes : (r + 1) * planes, h * LANES : (h + 1) * LANES]
            out[place] = jnp.where(lane < half, piece, listed).astype(bf16)
            out[place + 1] = jnp.where(lane < half, pltpu.roll(piece, half, 1), listed).astype(bf16)
            place += 2


def weigh_body(block, first_row, defocus, groups, bin_planes, bin_tilts, received, images, out, square, chosen, centre, tilt, table, mixer, held, power):
    _, rows, cols = images.shape
    group_total = table.shape[0]

    @pl.when(pl.program_id(0) == 0)
    def _():
        row = (lax.broadcasted_iota(jnp.int32, (rows, cols), 0) + first_row[0]).astype(f32)
        col = lax.broadcasted_iota(jnp.int32, (rows, cols), 1).astype(f32)
        row_freq = (row - cols // 2) * (2.0 / cols)
        col_freq = (col - cols // 2) * (2.0 / cols)
        radius = 0.5 * (row_freq * row_freq + col_freq * col_freq)

        def one(g, _):
            value = minus_sine_pi(radius * defocus[g] + phase_offset)
            table[g] = value
            value = value * value
            high = value.astype(bf16)
            power[0, g] = high
            power[1, g] = (value - high.astype(f32)).astype(bf16)
            return 0

        lax.fori_loop(0, group_total, one, 0, unroll=4)
        size = mixer.shape[0]
        here = lax.broadcasted_iota(jnp.int32, (size, size), 0)
        there = lax.broadcasted_iota(jnp.int32, (size, size), 1)
        mixer[...] = one_hot((here % rows) * rows + here // rows == there)
        for part in range(2):
            for g in range(0, group_total, rows):
                mixed = dot(mixer[...], power[part, g : g + rows].reshape(rows * rows, cols), ((1,), (0,)))
                square[:, part, g : g + rows, :] = mixed.astype(bf16).reshape(rows, rows, cols)
        chosen[...] = received[...]
        for q in range(centre.shape[0]):
            centre[q : q + 1, :] = jnp.full((1, LANES), bin_planes[q].astype(f32))
            tilt[q : q + 1, :] = jnp.full((1, LANES), bin_tilts[q])

    base = pl.program_id(0) * block

    def some(k, _):
        for m in range(rows):
            n = k * rows + m
            held[m] = (images[n].astype(f32) * table[groups[base + n]]).astype(bf16)
        mixed = dot(mixer[...], held[...].reshape(rows * rows, cols), ((1,), (0,)))
        out[:, pl.ds(k * rows, rows), :] = mixed.astype(bf16).reshape(rows, rows, cols)
        return 0

    lax.fori_loop(0, block // rows, some, 0, unroll=True)


def template_body(strip, height, row, centre, tilt, received, planes, out):
    bands = planes.shape[0]
    slab = planes.shape[1] // 2
    bins = centre.shape[0]
    total = bands * slab
    where = lax.broadcasted_iota(jnp.int32, (bins, total), 1).astype(f32)
    tables = []
    for h in range(2):
        deep = centre[...] + tilt[...] * reach_of(row[0] + h * strip, slab, height)
        deep = jnp.concatenate([deep] * (total // LANES), axis=1)
        weight = jnp.maximum(0.0, 1.0 - jnp.abs(where - deep)).astype(bf16)
        tables.append(dot(weight, planes[:, h * slab : (h + 1) * slab, :].reshape(total, LANES), ((1,), (0,))))
    lane = lax.broadcasted_iota(jnp.int32, (bins, LANES), 1)
    table = jnp.where(lane < LANES // 2, tables[0], pltpu.roll(tables[1], LANES // 2, 1))
    table = jnp.concatenate([jnp.zeros((LANES - bins, LANES), bf16), table.astype(bf16)], axis=0)
    chosen = received[...].reshape(-1, LANES)
    out[...] = dot(chosen, table, ((1,), (0,))).astype(bf16).reshape(out.shape)


top = 32767.0


def level_code(largest):
    code = jnp.floor(256.0 * jnp.log2(jnp.maximum(largest, 1e-30))) + 2.0
    return code, jnp.exp2(code * (-1.0 / 256.0))


def level_of(code):
    return jnp.exp2(code * (1.0 / 256.0))


def diagonal(count):
    shape = (count, LANES)
    return lax.broadcasted_iota(jnp.int32, shape, 0) == lax.broadcasted_iota(jnp.int32, shape, 1)


def score_body(templates, weighted, square, out, extra):
    rows, images, cols = weighted.shape
    group_total = square.shape[0]
    listed = templates.shape[1]
    total = None
    power = None
    lane = lax.broadcasted_iota(jnp.int32, (listed, LANES), 1)
    pieces = [None] * rows
    strip = rows // 2
    half = LANES // 2
    for r in range(strip):
        parts = [templates[4 * r + k].astype(f32) for k in range(4)]
        turned = [pltpu.roll(part, half, 1) for part in parts]
        pieces[r] = [jnp.where(lane < half, parts[k], turned[k + 1]) for k in (0, 2)]
        pieces[strip + r] = [jnp.where(lane < half, turned[k], parts[k + 1]) for k in (0, 2)]
    for r in range(rows):
        piece = jnp.concatenate(pieces[r], axis=1).astype(bf16)
        part = dot(piece, weighted[r], ((1,), (1,)))
        total = part if total is None else total + part
        wide = piece.astype(f32)
        wide = wide * wide
        high = wide.astype(bf16)
        low = (wide - high.astype(f32)).astype(bf16)
        left = jnp.concatenate([high, high, low], axis=1)
        right = jnp.concatenate([square[r, 0], square[r, 1], square[r, 0]], axis=1)
        part = dot(left, right, ((1,), (1,)))
        power = part if power is None else power + part
    group_total = power.shape[1]
    extra[...] = jnp.zeros_like(extra)
    extra[:, :group_total] = power
    power = jnp.maximum(extra[...], 0.0)
    row_code, row_scale = level_code(jnp.max(jnp.abs(total), axis=1, keepdims=True))
    total = total * row_scale
    image_code, image_scale = level_code(jnp.max(jnp.abs(total), axis=0, keepdims=True))
    total = jnp.clip(jnp.floor(total * image_scale * top + 0.5), -top, top)
    power_code, power_scale = level_code(jnp.max(power, axis=1, keepdims=True))
    power = jnp.minimum(power * power_scale, 1.0) * top
    high = jnp.floor(power)
    low = jnp.floor((power - high) * top + 0.5)
    half = listed // 2
    extra[:half] = (
        high[:half]
        + pltpu.roll(high[half:], group_total, 1)
        + pltpu.roll(low[:half], 2 * group_total, 1)
        + pltpu.roll(low[half:], 3 * group_total, 1)
    )
    chunks = images // LANES
    for c in range(chunks):
        extra[half + c : half + c + 1, :] = image_code[:, c * LANES : (c + 1) * LANES]
    square_mask = diagonal(listed)
    for place, code in ((half + chunks, row_code), (half + chunks + 1, power_code)):
        extra[place : place + 1, :] = jnp.sum(jnp.where(square_mask, code, 0.0), axis=0, keepdims=True)
    extra[half + chunks + 2 :, :] = jnp.zeros((listed - half - chunks - 2, LANES), f32)
    pieces = [total[:, c * LANES : (c + 1) * LANES] for c in range(chunks)] + [extra[...]]
    pieces = [piece.astype(jnp.int32).astype(jnp.int16) for piece in pieces]
    for k in range(out.shape[0]):
        for c, piece in enumerate(pieces):
            out[k, c * listed : (c + 1) * listed, :] = piece


def posterior_body(group_total, partial, groups, sharpness, weighted, posteriors, out):
    listed, images = posteriors.shape
    rows, _, cols = weighted.shape
    chunks = images // LANES
    half = listed // 2
    square_mask = diagonal(listed)
    lane = lax.broadcasted_iota(jnp.int32, (half, LANES), 1)
    scores = None
    power = None
    for k in range(partial.shape[0]):
        value = partial[k].astype(jnp.int32).astype(f32)
        extra = value[chunks * listed :]
        row_level, power_level = (
            level_of(jnp.sum(jnp.where(square_mask, extra[place : place + 1], 0.0), axis=1, keepdims=True)) / top
            for place in (half + chunks, half + chunks + 1)
        )
        image_level = [level_of(extra[half + c : half + c + 1]) for c in range(chunks)]
        part = [value[c * listed : (c + 1) * listed] * row_level * image_level[c] for c in range(chunks)]
        scores = part if scores is None else [a + b for a, b in zip(scores, part)]
        part = extra[:half] + pltpu.roll(extra[:half], LANES - 2 * group_total, 1) * (1.0 / top)
        part = part * jnp.where(lane < group_total, power_level[:half], power_level[half:])
        power = part if power is None else power + part
    scores = jnp.concatenate(scores, axis=1)
    power = jnp.where(lane < 2 * group_total, power, 0.0)
    scale = 1.0 / jnp.sqrt(power + epsilon)
    scale = jnp.concatenate([scale, pltpu.roll(scale, LANES - group_total, 1)], axis=0)
    member = lax.broadcasted_iota(jnp.int32, (LANES, images), 0) == groups[...]
    member = member.astype(f32)
    picked = lax.dot_general(
        scale, member, (((1,), (0,)), ((), ())), precision=lax.Precision.HIGHEST, preferred_element_type=f32
    )
    logits = sharpness[...] * scores * picked
    logits = jnp.exp(logits - jnp.max(logits, axis=0, keepdims=True))
    result = logits / jnp.sum(logits, axis=0, keepdims=True)
    posteriors[...] = result
    rounded = result.astype(bf16)
    totals = [dot(rounded, weighted[r], ((1,), (0,))) for r in range(rows)]
    for h in range(cols // LANES):
        parts = [total[:, h * LANES : (h + 1) * LANES] for total in totals]
        parts = swap_blocks(parts, LANES // rows)
        for j in range(rows):
            out[h * rows + j] = parts[j].astype(bf16)


def project_body(rows, height, first_row, centre, tilt, received, arrived, out):
    bands, planes, _ = out.shape
    bins = centre.shape[0]
    pairs = arrived.shape[0] * arrived.shape[1]
    by_bin = dot(arrived[...].reshape(pairs, LANES), received[...].reshape(pairs, LANES), ((0,), (0,)))
    width = LANES // rows
    lane = lax.broadcasted_iota(jnp.int32, (bins, LANES), 1)
    empty = jnp.zeros((LANES - bins, 2 * LANES), bf16)
    parts = []
    for r in range(rows):
        deep = centre[...] + tilt[...] * reach_of(first_row[0] + r, planes, height)
        weights = []
        for h in range(2):
            where = ((lane % bands) * planes + h * (planes // 2) + lane // bands).astype(f32)
            weights.append(jnp.maximum(0.0, 1.0 - jnp.abs(where - deep)).astype(bf16))
        weight = jnp.concatenate([empty, jnp.concatenate(weights, axis=1)], axis=0)
        parts.append(dot(by_bin[r * width : (r + 1) * width].astype(bf16), weight, ((1,), (0,))))
    first = swap_blocks([part[:, :LANES] for part in parts], 1)
    second = swap_blocks([part[:, LANES:] for part in parts], 1)
    for j in range(bands):
        out[j] = jnp.concatenate([first[j], second[j]], axis=0).astype(bf16)


def final_body(arrived, out):
    bands = arrived.shape[0]
    wide = arrived[...].astype(f32)
    for zh in range(2):
        for vh in range(bands // 8):
            parts = [wide[vh * 8 + k, zh * 8 : (zh + 1) * 8, :] for k in range(8)]
            parts = swap_blocks(parts, LANES // 8)
            for zl in range(8):
                out[zh * 8 + zl, :, vh * LANES : (vh + 1) * LANES] = parts[zl]


def per_device(volume, images, bin_lists, bin_planes, bin_tilts, defocus, groups, precision):
    bands = lax.axis_size("vol")
    blocks = lax.axis_size("img")
    planes, strip, cols = volume.shape
    image_count, rows, _ = images.shape
    height = rows * bands
    bins = bin_planes.shape[0]
    listed = bin_lists.shape[1]
    group_total = defocus.shape[0]
    first_row = row_of(rows).reshape(1)

    sent = call(
        part_body,
        pltpu.VMEM((blocks, planes, LANES), bf16),
        [VMEM, VMEM],
        VMEM,
    )(*in_hbm(bin_lists, volume))
    received = lax.all_to_all(sent, "img", 0, 0, tiled=True)
    stack = lax.all_to_all(received.reshape(bands, 2 * planes, LANES), "vol", 0, 0, tiled=True)

    block = 256
    weighted, square, chosen, centre, tilt = call(
        functools.partial(weigh_body, block),
        (
            pltpu.HBM((rows, image_count, cols), bf16),
            jax.ShapeDtypeStruct((rows, 2, group_total, cols), bf16),
            jax.ShapeDtypeStruct((blocks, planes, LANES), bf16),
            jax.ShapeDtypeStruct((bins, LANES), f32),
            jax.ShapeDtypeStruct((bins, LANES), f32),
        ),
        [SMEM] * 5
        + [
            pl.BlockSpec((blocks, planes, LANES), lambda i: (0, 0, 0)),
            pl.BlockSpec((block, rows, cols), lambda i: (i, 0, 0)),
        ],
        (
            pl.BlockSpec((rows, block, cols), lambda i: (0, i, 0)),
            pl.BlockSpec((rows, 2, group_total, cols), lambda i: (0, 0, 0, 0)),
            pl.BlockSpec((blocks, planes, LANES), lambda i: (0, 0, 0)),
            pl.BlockSpec((bins, LANES), lambda i: (0, 0)),
            pl.BlockSpec((bins, LANES), lambda i: (0, 0)),
        ),
        scratch=(
            pltpu.VMEM((group_total, rows, cols), f32),
            pltpu.VMEM((rows * rows, rows * rows), bf16),
            pltpu.VMEM((rows, rows, cols), bf16),
            pltpu.VMEM((2, group_total, rows, cols), bf16),
        ),
        grid=(image_count // block,),
        flops=40 * image_count * rows * cols,
        nbytes=4 * image_count * rows * cols,
    )(first_row, *in_hbm(defocus, groups, bin_planes, bin_tilts, received, images))

    pieces = call(
        functools.partial(template_body, strip, height),
        jax.ShapeDtypeStruct((blocks, listed, LANES), bf16),
        [SMEM, VMEM, VMEM, VMEM, VMEM],
        VMEM,
        flops=2**33,
        nbytes=2**25,
    )(first_row + lax.axis_index("img") // 4, centre, tilt, chosen, stack)
    templates = lax.all_to_all(pieces, "img", 0, 0, tiled=True)

    payload_rows = listed * (image_count // LANES + 1)
    partial = call(
        score_body,
        jax.ShapeDtypeStruct((bands, payload_rows, LANES), jnp.int16),
        [VMEM, VMEM, VMEM],
        VMEM,
        scratch=(pltpu.VMEM((listed, LANES), f32),),
    )(templates, weighted, square)
    partial = lax.all_to_all(partial, "vol", 0, 0, tiled=True)

    posteriors, spread = call(
        functools.partial(posterior_body, group_total),
        (
            jax.ShapeDtypeStruct((listed, image_count), f32),
            jax.ShapeDtypeStruct((blocks, listed, LANES), bf16),
        ),
        [VMEM, VMEM, VMEM, VMEM],
        (VMEM, VMEM),
    )(partial, groups.reshape(1, image_count), precision.reshape(1, image_count), weighted)
    arrived = lax.all_to_all(spread, "img", 0, 0, tiled=True)

    projected = call(
        functools.partial(project_body, rows, height),
        jax.ShapeDtypeStruct((bands, planes, LANES), bf16),
        [SMEM, VMEM, VMEM, VMEM, VMEM],
        VMEM,
    )(first_row, centre, tilt, chosen, arrived)
    slabs = lax.all_to_all(projected, "vol", 0, 0, tiled=True)
    numerator = call(
        final_body,
        jax.ShapeDtypeStruct((planes, cols // blocks, height), f32),
        [VMEM],
        VMEM,
    )(slabs)
    return (posteriors.T, numerator.transpose(0, 2, 1))


def solution(mesh):
    placed = (
        P("vol", "img", None),
        P("img", "vol", None),
        P("img", None),
        P(),
        P(),
        P(),
        P("img"),
        P("img"),
    )
    return jax.shard_map(
        per_device,
        mesh=mesh,
        in_specs=placed,
        out_specs=(P("img", None), P("vol", None, "img")),
        check_vma=False,
    )
```

```python
import functools
import math

import jax
import jax.numpy as jnp
from jax import lax
from jax.experimental import pallas as pl
from jax.experimental.pallas import tpu as pltpu
from jax.sharding import PartitionSpec as P

phase_offset = math.asin(0.1) / math.pi
epsilon = 1e-05
bf16 = jnp.bfloat16
f32 = jnp.float32
LANES = 128
VMEM = pl.BlockSpec(memory_space=pltpu.VMEM)
SMEM = pl.BlockSpec(memory_space=pltpu.SMEM)


def call(body, out_shape, in_specs, out_specs, scratch=(), grid=(), flops=0, nbytes=0, vmem=16):
    return pl.pallas_call(
        body,
        out_shape=out_shape,
        grid=grid,
        in_specs=in_specs,
        out_specs=out_specs,
        scratch_shapes=list(scratch),
        cost_estimate=pl.CostEstimate(flops=flops, bytes_accessed=nbytes, transcendentals=0),
        compiler_params=pltpu.CompilerParams(vmem_limit_bytes=vmem * 2**20),
    )


def in_hbm(*arrays):
    return [pltpu.with_memory_space_constraint(array, pltpu.HBM) for array in arrays]


def dot(a, b, contract):
    return lax.dot_general(a, b, ((contract[0], contract[1]), ((), ())), preferred_element_type=f32)


def minus_sine_pi(turns):
    whole = jnp.floor(turns + 0.5)
    rest = turns - whole
    odd = whole - 2.0 * jnp.floor(whole * 0.5)
    x = rest * math.pi
    square = x * x
    total = -1.0 / 39916800.0
    for term in (1.0 / 362880.0, -1.0 / 5040.0, 1.0 / 120.0, -1.0 / 6.0, 1.0):
        total = total * square + term
    return total * x * (2.0 * odd - 1.0)


def swap_blocks(parts, stride):
    count = len(parts)
    lane = lax.broadcasted_iota(jnp.int32, parts[0].shape, parts[0].ndim - 1)
    bit = 1
    while bit < count:
        shift = stride * bit
        low = (lane & shift) == 0
        axis = parts[0].ndim - 1
        result = list(parts)
        for i in range(count):
            if i & bit:
                continue
            a, c = parts[i], parts[i | bit]
            result[i] = jnp.where(low, a, pltpu.roll(c, shift, axis))
            result[i | bit] = jnp.where(low, pltpu.roll(a, LANES - shift, axis), c)
        parts = result
        bit *= 2
    return parts


def row_of(rows):
    return lax.axis_index("vol") * rows


def reach_of(row, planes, height):
    return float(planes) * ((row.astype(f32) - (height - 1) * 0.5) * (2.0 / height))


def one_hot(mask):
    return mask.astype(f32).astype(bf16)


def part_body(lists, volume, out):
    planes, strip, cols = volume.shape
    size = planes * strip
    here = lax.broadcasted_iota(jnp.int32, (size, size), 0)
    there = lax.broadcasted_iota(jnp.int32, (size, size), 1)
    mixer = one_hot((here % planes) * strip + here // planes == there)
    mixed = dot(mixer, volume[...].astype(f32).reshape(size, cols).astype(bf16), ((1,), (0,)))
    lane = lax.broadcasted_iota(jnp.int32, (planes, LANES), 1)
    half = LANES // 2
    ids = jnp.concatenate([lists[...], jnp.zeros((1, LANES - planes), jnp.int32)], axis=1)
    ids = jnp.sum(jnp.where(diagonal(planes), ids, 0), axis=1, keepdims=True)
    listed = (lane == ids + half).astype(f32)
    place = 0
    for r in range(strip):
        for h in range(cols // LANES):
            piece = mixed[r * planes : (r + 1) * planes, h * LANES : (h + 1) * LANES]
            out[place] = jnp.where(lane < half, piece, listed).astype(bf16)
            out[place + 1] = jnp.where(lane < half, pltpu.roll(piece, half, 1), listed).astype(bf16)
            place += 2


def weigh_body(block, first_row, defocus, groups, bin_planes, bin_tilts, received, images, out, square, chosen, centre, tilt, table, mixer, held, power):
    _, rows, cols = images.shape
    group_total = table.shape[0]

    @pl.when(pl.program_id(0) == 0)
    def _():
        row = (lax.broadcasted_iota(jnp.int32, (rows, cols), 0) + first_row[0]).astype(f32)
        col = lax.broadcasted_iota(jnp.int32, (rows, cols), 1).astype(f32)
        row_freq = (row - cols // 2) * (2.0 / cols)
        col_freq = (col - cols // 2) * (2.0 / cols)
        radius = 0.5 * (row_freq * row_freq + col_freq * col_freq)

        def one(g, _):
            value = minus_sine_pi(radius * defocus[g] + phase_offset)
            table[g] = value
            value = value * value
            high = value.astype(bf16)
            power[0, g] = high
            power[1, g] = (value - high.astype(f32)).astype(bf16)
            return 0

        lax.fori_loop(0, group_total, one, 0, unroll=4)
        size = mixer.shape[0]
        here = lax.broadcasted_iota(jnp.int32, (size, size), 0)
        there = lax.broadcasted_iota(jnp.int32, (size, size), 1)
        mixer[...] = one_hot((here % rows) * rows + here // rows == there)
        for part in range(2):
            for g in range(0, group_total, rows):
                mixed = dot(mixer[...], power[part, g : g + rows].reshape(rows * rows, cols), ((1,), (0,)))
                square[:, part, g : g + rows, :] = mixed.astype(bf16).reshape(rows, rows, cols)
        chosen[...] = received[...]
        for q in range(centre.shape[0]):
            centre[q : q + 1, :] = jnp.full((1, LANES), bin_planes[q].astype(f32))
            tilt[q : q + 1, :] = jnp.full((1, LANES), bin_tilts[q])

    base = pl.program_id(0) * block

    def some(k, _):
        for m in range(rows):
            n = k * rows + m
            held[m] = (images[n].astype(f32) * table[groups[base + n]]).astype(bf16)
        mixed = dot(mixer[...], held[...].reshape(rows * rows, cols), ((1,), (0,)))
        out[:, pl.ds(k * rows, rows), :] = mixed.astype(bf16).reshape(rows, rows, cols)
        return 0

    lax.fori_loop(0, block // rows, some, 0, unroll=True)


def template_body(strip, height, row, centre, tilt, received, planes, out):
    bands = planes.shape[0]
    slab = planes.shape[1] // 2
    bins = centre.shape[0]
    total = bands * slab
    where = lax.broadcasted_iota(jnp.int32, (bins, total), 1).astype(f32)
    tables = []
    for h in range(2):
        deep = centre[...] + tilt[...] * reach_of(row[0] + h * strip, slab, height)
        deep = jnp.concatenate([deep] * (total // LANES), axis=1)
        weight = jnp.maximum(0.0, 1.0 - jnp.abs(where - deep)).astype(bf16)
        tables.append(dot(weight, planes[:, h * slab : (h + 1) * slab, :].reshape(total, LANES), ((1,), (0,))))
    lane = lax.broadcasted_iota(jnp.int32, (bins, LANES), 1)
    table = jnp.where(lane < LANES // 2, tables[0], pltpu.roll(tables[1], LANES // 2, 1))
    table = jnp.concatenate([jnp.zeros((LANES - bins, LANES), bf16), table.astype(bf16)], axis=0)
    chosen = received[...].reshape(-1, LANES)
    out[...] = dot(chosen, table, ((1,), (0,))).astype(bf16).reshape(out.shape)


top = 32767.0


def level_code(largest):
    return jnp.floor(256.0 * jnp.log2(jnp.maximum(largest, 1e-30))) + 2.0


def level_of(code):
    return jnp.exp2(code * (1.0 / 256.0))


def diagonal(count):
    shape = (count, LANES)
    return lax.broadcasted_iota(jnp.int32, shape, 0) == lax.broadcasted_iota(jnp.int32, shape, 1)


def score_body(templates, weighted, square, out, extra):
    rows, images, cols = weighted.shape
    group_total = square.shape[0]
    listed = templates.shape[1]
    total = None
    power = None
    lane = lax.broadcasted_iota(jnp.int32, (listed, LANES), 1)
    pieces = [None] * rows
    strip = rows // 2
    half = LANES // 2
    for r in range(strip):
        parts = [templates[4 * r + k].astype(f32) for k in range(4)]
        turned = [pltpu.roll(part, half, 1) for part in parts]
        pieces[r] = [jnp.where(lane < half, parts[k], turned[k + 1]) for k in (0, 2)]
        pieces[strip + r] = [jnp.where(lane < half, turned[k], parts[k + 1]) for k in (0, 2)]
    for r in range(rows):
        piece = jnp.concatenate(pieces[r], axis=1).astype(bf16)
        part = dot(piece, weighted[r], ((1,), (1,)))
        total = part if total is None else total + part
        wide = piece.astype(f32)
        wide = wide * wide
        high = wide.astype(bf16)
        low = (wide - high.astype(f32)).astype(bf16)
        left = jnp.concatenate([high, high, low], axis=1)
        right = jnp.concatenate([square[r, 0], square[r, 1], square[r, 0]], axis=1)
        part = dot(left, right, ((1,), (1,)))
        power = part if power is None else power + part
    group_total = power.shape[1]
    extra[...] = jnp.zeros_like(extra)
    extra[:, :group_total] = power
    power = jnp.maximum(extra[...], 0.0)
    power_code = level_code(jnp.max(power, axis=1, keepdims=True))
    power = jnp.minimum(power * level_of(-power_code), 1.0) * top
    total = total * level_of(-0.5 * power_code)
    image_code = level_code(jnp.max(jnp.abs(total), axis=0, keepdims=True))
    total = jnp.clip(jnp.floor(total * level_of(-image_code) * top + 0.5), -top, top)
    high = jnp.floor(power)
    low = jnp.floor((power - high) * top + 0.5)
    half = listed // 2
    extra[:half] = (
        high[:half]
        + pltpu.roll(high[half:], group_total, 1)
        + pltpu.roll(low[:half], 2 * group_total, 1)
        + pltpu.roll(low[half:], 3 * group_total, 1)
    )
    chunks = images // LANES
    for c in range(chunks):
        extra[half + c : half + c + 1, :] = image_code[:, c * LANES : (c + 1) * LANES]
    square_mask = diagonal(listed)
    place = half + chunks
    extra[place : place + 1, :] = jnp.sum(jnp.where(square_mask, power_code, 0.0), axis=0, keepdims=True)
    extra[place + 1 :, :] = jnp.zeros((listed - place - 1, LANES), f32)
    pieces = [total[:, c * LANES : (c + 1) * LANES] for c in range(chunks)] + [extra[...]]
    pieces = [piece.astype(jnp.int32).astype(jnp.int16) for piece in pieces]
    for k in range(out.shape[0]):
        for c, piece in enumerate(pieces):
            out[k, c * listed : (c + 1) * listed, :] = piece


def posterior_body(group_total, partial, groups, sharpness, weighted, posteriors, out):
    listed, images = posteriors.shape
    rows, _, cols = weighted.shape
    chunks = images // LANES
    half = listed // 2
    square_mask = diagonal(listed)
    lane = lax.broadcasted_iota(jnp.int32, (half, LANES), 1)
    scores = None
    power = None
    for k in range(partial.shape[0]):
        value = partial[k].astype(jnp.int32).astype(f32)
        extra = value[chunks * listed :]
        place = half + chunks
        power_code = jnp.sum(jnp.where(square_mask, extra[place : place + 1], 0.0), axis=1, keepdims=True)
        row_level = level_of(0.5 * power_code) * (1.0 / top)
        power_level = level_of(power_code) * (1.0 / top)
        image_level = [level_of(extra[half + c : half + c + 1]) for c in range(chunks)]
        part = [value[c * listed : (c + 1) * listed] * row_level * image_level[c] for c in range(chunks)]
        scores = part if scores is None else [a + b for a, b in zip(scores, part)]
        part = extra[:half] + pltpu.roll(extra[:half], LANES - 2 * group_total, 1) * (1.0 / top)
        part = part * jnp.where(lane < group_total, power_level[:half], power_level[half:])
        power = part if power is None else power + part
    scores = jnp.concatenate(scores, axis=1)
    power = jnp.where(lane < 2 * group_total, power, 0.0)
    scale = 1.0 / jnp.sqrt(power + epsilon)
    scale = jnp.concatenate([scale, pltpu.roll(scale, LANES - group_total, 1)], axis=0)
    member = lax.broadcasted_iota(jnp.int32, (LANES, images), 0) == groups[...]
    member = member.astype(f32)
    picked = lax.dot_general(
        scale, member, (((1,), (0,)), ((), ())), precision=lax.Precision.HIGHEST, preferred_element_type=f32
    )
    logits = sharpness[...] * scores * picked
    logits = jnp.exp(logits - jnp.max(logits, axis=0, keepdims=True))
    result = logits / jnp.sum(logits, axis=0, keepdims=True)
    posteriors[...] = result
    rounded = result.astype(bf16)
    totals = [dot(rounded, weighted[r], ((1,), (0,))) for r in range(rows)]
    for h in range(cols // LANES):
        parts = [total[:, h * LANES : (h + 1) * LANES] for total in totals]
        parts = swap_blocks(parts, LANES // rows)
        for j in range(rows):
            out[h * rows + j] = parts[j].astype(bf16)


def project_body(rows, height, first_row, centre, tilt, received, arrived, out):
    bands, planes, _ = out.shape
    bins = centre.shape[0]
    pairs = arrived.shape[0] * arrived.shape[1]
    by_bin = dot(arrived[...].reshape(pairs, LANES), received[...].reshape(pairs, LANES), ((0,), (0,)))
    width = LANES // rows
    lane = lax.broadcasted_iota(jnp.int32, (bins, LANES), 1)
    empty = jnp.zeros((LANES - bins, 2 * LANES), bf16)
    parts = []
    for r in range(rows):
        deep = centre[...] + tilt[...] * reach_of(first_row[0] + r, planes, height)
        weights = []
        for h in range(2):
            where = ((lane % bands) * planes + h * (planes // 2) + lane // bands).astype(f32)
            weights.append(jnp.maximum(0.0, 1.0 - jnp.abs(where - deep)).astype(bf16))
        weight = jnp.concatenate([empty, jnp.concatenate(weights, axis=1)], axis=0)
        parts.append(dot(by_bin[r * width : (r + 1) * width].astype(bf16), weight, ((1,), (0,))))
    first = swap_blocks([part[:, :LANES] for part in parts], 1)
    second = swap_blocks([part[:, LANES:] for part in parts], 1)
    for j in range(bands):
        out[j] = jnp.concatenate([first[j], second[j]], axis=0).astype(bf16)


def final_body(arrived, out):
    bands = arrived.shape[0]
    wide = arrived[...].astype(f32)
    for zh in range(2):
        for vh in range(bands // 8):
            parts = [wide[vh * 8 + k, zh * 8 : (zh + 1) * 8, :] for k in range(8)]
            parts = swap_blocks(parts, LANES // 8)
            for zl in range(8):
                out[zh * 8 + zl, :, vh * LANES : (vh + 1) * LANES] = parts[zl]


def per_device(volume, images, bin_lists, bin_planes, bin_tilts, defocus, groups, precision):
    bands = lax.axis_size("vol")
    blocks = lax.axis_size("img")
    planes, strip, cols = volume.shape
    image_count, rows, _ = images.shape
    height = rows * bands
    bins = bin_planes.shape[0]
    listed = bin_lists.shape[1]
    group_total = defocus.shape[0]
    first_row = row_of(rows).reshape(1)

    sent = call(
        part_body,
        pltpu.VMEM((blocks, planes, LANES), bf16),
        [VMEM, VMEM],
        VMEM,
    )(*in_hbm(bin_lists, volume))
    received = lax.all_to_all(sent, "img", 0, 0, tiled=True)
    stack = lax.all_to_all(received.reshape(bands, 2 * planes, LANES), "vol", 0, 0, tiled=True)

    block = 256
    weighted, square, chosen, centre, tilt = call(
        functools.partial(weigh_body, block),
        (
            pltpu.HBM((rows, image_count, cols), bf16),
            jax.ShapeDtypeStruct((rows, 2, group_total, cols), bf16),
            jax.ShapeDtypeStruct((blocks, planes, LANES), bf16),
            jax.ShapeDtypeStruct((bins, LANES), f32),
            jax.ShapeDtypeStruct((bins, LANES), f32),
        ),
        [SMEM] * 5
        + [
            pl.BlockSpec((blocks, planes, LANES), lambda i: (0, 0, 0)),
            pl.BlockSpec((block, rows, cols), lambda i: (i, 0, 0)),
        ],
        (
            pl.BlockSpec((rows, block, cols), lambda i: (0, i, 0)),
            pl.BlockSpec((rows, 2, group_total, cols), lambda i: (0, 0, 0, 0)),
            pl.BlockSpec((blocks, planes, LANES), lambda i: (0, 0, 0)),
            pl.BlockSpec((bins, LANES), lambda i: (0, 0)),
            pl.BlockSpec((bins, LANES), lambda i: (0, 0)),
        ),
        scratch=(
            pltpu.VMEM((group_total, rows, cols), f32),
            pltpu.VMEM((rows * rows, rows * rows), bf16),
            pltpu.VMEM((rows, rows, cols), bf16),
            pltpu.VMEM((2, group_total, rows, cols), bf16),
        ),
        grid=(image_count // block,),
        flops=40 * image_count * rows * cols,
        nbytes=4 * image_count * rows * cols,
    )(first_row, *in_hbm(defocus, groups, bin_planes, bin_tilts, received, images))

    pieces = call(
        functools.partial(template_body, strip, height),
        jax.ShapeDtypeStruct((blocks, listed, LANES), bf16),
        [SMEM, VMEM, VMEM, VMEM, VMEM],
        VMEM,
        flops=2**33,
        nbytes=2**25,
    )(first_row + lax.axis_index("img") // 4, centre, tilt, chosen, stack)
    templates = lax.all_to_all(pieces, "img", 0, 0, tiled=True)

    payload_rows = listed * (image_count // LANES + 1)
    partial = call(
        score_body,
        jax.ShapeDtypeStruct((bands, payload_rows, LANES), jnp.int16),
        [VMEM, VMEM, VMEM],
        VMEM,
        scratch=(pltpu.VMEM((listed, LANES), f32),),
    )(templates, weighted, square)
    partial = lax.all_to_all(partial, "vol", 0, 0, tiled=True)

    posteriors, spread = call(
        functools.partial(posterior_body, group_total),
        (
            jax.ShapeDtypeStruct((listed, image_count), f32),
            jax.ShapeDtypeStruct((blocks, listed, LANES), bf16),
        ),
        [VMEM, VMEM, VMEM, VMEM],
        (VMEM, VMEM),
    )(partial, groups.reshape(1, image_count), precision.reshape(1, image_count), weighted)
    arrived = lax.all_to_all(spread, "img", 0, 0, tiled=True)

    projected = call(
        functools.partial(project_body, rows, height),
        jax.ShapeDtypeStruct((bands, planes, LANES), bf16),
        [SMEM, VMEM, VMEM, VMEM, VMEM],
        VMEM,
    )(first_row, centre, tilt, chosen, arrived)
    slabs = lax.all_to_all(projected, "vol", 0, 0, tiled=True)
    numerator = call(
        final_body,
        jax.ShapeDtypeStruct((planes, cols // blocks, height), f32),
        [VMEM],
        VMEM,
    )(slabs)
    return (posteriors.T, numerator.transpose(0, 2, 1))


def solution(mesh):
    placed = (
        P("vol", "img", None),
        P("img", "vol", None),
        P("img", None),
        P(),
        P(),
        P(),
        P("img"),
        P("img"),
    )
    return jax.shard_map(
        per_device,
        mesh=mesh,
        in_specs=placed,
        out_specs=(P("img", None), P("vol", None, "img")),
        check_vma=False,
    )
```

```python
import functools
import math

import jax
import jax.numpy as jnp
from jax import lax
from jax.experimental import pallas as pl
from jax.experimental.pallas import tpu as pltpu
from jax.sharding import PartitionSpec as P

phase_offset = math.asin(0.1) / math.pi
epsilon = 1e-05
bf16 = jnp.bfloat16
f32 = jnp.float32
LANES = 128
VMEM = pl.BlockSpec(memory_space=pltpu.VMEM)
SMEM = pl.BlockSpec(memory_space=pltpu.SMEM)


def call(body, out_shape, in_specs, out_specs, scratch=(), grid=(), flops=0, nbytes=0, vmem=16):
    return pl.pallas_call(
        body,
        out_shape=out_shape,
        grid=grid,
        in_specs=in_specs,
        out_specs=out_specs,
        scratch_shapes=list(scratch),
        cost_estimate=pl.CostEstimate(flops=flops, bytes_accessed=nbytes, transcendentals=0),
        compiler_params=pltpu.CompilerParams(vmem_limit_bytes=vmem * 2**20),
    )


def in_hbm(*arrays):
    return [pltpu.with_memory_space_constraint(array, pltpu.HBM) for array in arrays]


def dot(a, b, contract):
    return lax.dot_general(a, b, ((contract[0], contract[1]), ((), ())), preferred_element_type=f32)


def minus_sine_pi(turns):
    whole = jnp.floor(turns + 0.5)
    rest = turns - whole
    odd = whole - 2.0 * jnp.floor(whole * 0.5)
    x = rest * math.pi
    square = x * x
    total = -1.0 / 39916800.0
    for term in (1.0 / 362880.0, -1.0 / 5040.0, 1.0 / 120.0, -1.0 / 6.0, 1.0):
        total = total * square + term
    return total * x * (2.0 * odd - 1.0)


def swap_blocks(parts, stride):
    count = len(parts)
    lane = lax.broadcasted_iota(jnp.int32, parts[0].shape, parts[0].ndim - 1)
    bit = 1
    while bit < count:
        shift = stride * bit
        low = (lane & shift) == 0
        axis = parts[0].ndim - 1
        result = list(parts)
        for i in range(count):
            if i & bit:
                continue
            a, c = parts[i], parts[i | bit]
            result[i] = jnp.where(low, a, pltpu.roll(c, shift, axis))
            result[i | bit] = jnp.where(low, pltpu.roll(a, LANES - shift, axis), c)
        parts = result
        bit *= 2
    return parts


def row_of(rows):
    return lax.axis_index("vol") * rows


def reach_of(row, planes, height):
    return float(planes) * ((row.astype(f32) - (height - 1) * 0.5) * (2.0 / height))


def one_hot(mask):
    return mask.astype(f32).astype(bf16)


def part_body(lists, volume, out):
    planes, strip, cols = volume.shape
    listed = lists.shape[1]
    size = planes * strip
    here = lax.broadcasted_iota(jnp.int32, (size, size), 0)
    there = lax.broadcasted_iota(jnp.int32, (size, size), 1)
    mixer = one_hot((here % planes) * strip + here // planes == there)
    mixed = dot(mixer, volume[...].astype(f32).reshape(size, cols).astype(bf16), ((1,), (0,)))
    ids = jnp.concatenate([lists[...], jnp.zeros((1, LANES - listed), jnp.int32)], axis=1)
    ids = jnp.sum(jnp.where(diagonal(listed), ids, 0), axis=1, keepdims=True)
    lane = lax.broadcasted_iota(jnp.int32, (listed // 2, LANES), 1)
    half = LANES // 2
    hit = lane == jnp.where(lane < half, ids[: listed // 2], ids[listed // 2 :] + half)
    marked = hit.astype(f32)
    place = 0
    for r in range(strip):
        for h in range(cols // LANES):
            piece = mixed[r * planes : (r + 1) * planes, h * LANES : (h + 1) * LANES]
            piece = jnp.concatenate([piece, marked], axis=0).astype(bf16)
            out[place] = piece
            out[out.shape[0] // 2 + place] = piece
            place += 1


def weigh_body(block, first_row, defocus, groups, bin_planes, bin_tilts, received, images, out, square, chosen, centre, tilt, table, mixer, held, power):
    _, rows, cols = images.shape
    group_total = table.shape[0]

    @pl.when(pl.program_id(0) == 0)
    def _():
        row = (lax.broadcasted_iota(jnp.int32, (rows, cols), 0) + first_row[0]).astype(f32)
        col = lax.broadcasted_iota(jnp.int32, (rows, cols), 1).astype(f32)
        row_freq = (row - cols // 2) * (2.0 / cols)
        col_freq = (col - cols // 2) * (2.0 / cols)
        radius = 0.5 * (row_freq * row_freq + col_freq * col_freq)

        def one(g, _):
            value = minus_sine_pi(radius * defocus[g] + phase_offset)
            table[g] = value
            value = value * value
            high = value.astype(bf16)
            power[0, g] = high
            power[1, g] = (value - high.astype(f32)).astype(bf16)
            return 0

        lax.fori_loop(0, group_total, one, 0, unroll=4)
        size = mixer.shape[0]
        here = lax.broadcasted_iota(jnp.int32, (size, size), 0)
        there = lax.broadcasted_iota(jnp.int32, (size, size), 1)
        mixer[...] = one_hot((here % rows) * rows + here // rows == there)
        for part in range(2):
            for g in range(0, group_total, rows):
                mixed = dot(mixer[...], power[part, g : g + rows].reshape(rows * rows, cols), ((1,), (0,)))
                square[:, part, g : g + rows, :] = mixed.astype(bf16).reshape(rows, rows, cols)
        marked = received[...].astype(f32)[:, chosen.shape[1] :, :]
        chosen[...] = jnp.concatenate([pltpu.roll(marked, LANES // 2, 2), marked], axis=1).astype(bf16)
        for q in range(centre.shape[0]):
            centre[q : q + 1, :] = jnp.full((1, LANES), bin_planes[q].astype(f32))
            tilt[q : q + 1, :] = jnp.full((1, LANES), bin_tilts[q])

    base = pl.program_id(0) * block

    def some(k, _):
        for m in range(rows):
            n = k * rows + m
            held[m] = (images[n].astype(f32) * table[groups[base + n]]).astype(bf16)
        mixed = dot(mixer[...], held[...].reshape(rows * rows, cols), ((1,), (0,)))
        out[:, pl.ds(k * rows, rows), :] = mixed.astype(bf16).reshape(rows, rows, cols)
        return 0

    lax.fori_loop(0, block // rows, some, 0, unroll=True)


def template_body(strip, slab, height, row, group, centre, tilt, chosen, planes, out):
    bands, both, _ = planes.shape
    bins = centre.shape[0]
    peers, listed = out.shape[0], out.shape[1] // 2
    total = bands * slab
    where = lax.broadcasted_iota(jnp.int32, (bins, total), 1).astype(f32)
    picker = chosen[pl.ds(group[0] * peers, peers)].reshape(peers * listed, LANES)
    values = planes[...].astype(f32)
    empty = jnp.zeros((LANES - bins, LANES), bf16)
    for h in range(2):
        deep = centre[...] + tilt[...] * reach_of(row[0] + h * strip, slab, height)
        deep = jnp.concatenate([deep] * (total // LANES), axis=1)
        weight = jnp.maximum(0.0, 1.0 - jnp.abs(where - deep)).astype(bf16)
        start = h * (both // 2)
        rows = values[:, start : start + slab, :].reshape(total, LANES).astype(bf16)
        table = jnp.concatenate([empty, dot(weight, rows, ((1,), (0,))).astype(bf16)], axis=0)
        picked = dot(picker, table, ((1,), (0,))).astype(bf16)
        out[:, h * listed : (h + 1) * listed, :] = picked.reshape(peers, listed, LANES)


top = 32767.0


def level_code(largest):
    return jnp.floor(256.0 * jnp.log2(jnp.maximum(largest, 1e-30))) + 2.0


def level_of(code):
    return jnp.exp2(code * (1.0 / 256.0))


def diagonal(count):
    shape = (count, LANES)
    return lax.broadcasted_iota(jnp.int32, shape, 0) == lax.broadcasted_iota(jnp.int32, shape, 1)


def score_body(templates, weighted, square, out, extra):
    rows, images, cols = weighted.shape
    group_total = square.shape[0]
    listed = templates.shape[1] // 2
    total = None
    power = None
    strip = rows // 2
    for r in range(rows):
        start = r // strip * listed
        piece = [templates[2 * (r % strip) + k, start : start + listed, :] for k in range(cols // LANES)]
        piece = jnp.concatenate(piece, axis=1)
        part = dot(piece, weighted[r], ((1,), (1,)))
        total = part if total is None else total + part
        wide = piece.astype(f32)
        wide = wide * wide
        high = wide.astype(bf16)
        low = (wide - high.astype(f32)).astype(bf16)
        left = jnp.concatenate([high, high, low], axis=1)
        right = jnp.concatenate([square[r, 0], square[r, 1], square[r, 0]], axis=1)
        part = dot(left, right, ((1,), (1,)))
        power = part if power is None else power + part
    group_total = power.shape[1]
    extra[...] = jnp.zeros_like(extra)
    extra[:, :group_total] = power
    power = jnp.maximum(extra[...], 0.0)
    power_code = level_code(jnp.max(power, axis=1, keepdims=True))
    power = jnp.minimum(power * level_of(-power_code), 1.0) * top
    total = total * level_of(-0.5 * power_code)
    image_code = level_code(jnp.max(jnp.abs(total), axis=0, keepdims=True))
    total = jnp.clip(jnp.floor(total * level_of(-image_code) * top + 0.5), -top, top)
    high = jnp.floor(power)
    low = jnp.floor((power - high) * top + 0.5)
    half = listed // 2
    extra[:half] = (
        high[:half]
        + pltpu.roll(high[half:], group_total, 1)
        + pltpu.roll(low[:half], 2 * group_total, 1)
        + pltpu.roll(low[half:], 3 * group_total, 1)
    )
    chunks = images // LANES
    for c in range(chunks):
        extra[half + c : half + c + 1, :] = image_code[:, c * LANES : (c + 1) * LANES]
    square_mask = diagonal(listed)
    place = half + chunks
    extra[place : place + 1, :] = jnp.sum(jnp.where(square_mask, power_code, 0.0), axis=0, keepdims=True)
    extra[place + 1 :, :] = jnp.zeros((listed - place - 1, LANES), f32)
    pieces = [total[:, c * LANES : (c + 1) * LANES] for c in range(chunks)] + [extra[...]]
    pieces = [piece.astype(jnp.int32).astype(jnp.int16) for piece in pieces]
    for k in range(out.shape[0]):
        for c, piece in enumerate(pieces):
            out[k, c * listed : (c + 1) * listed, :] = piece


def posterior_body(group_total, partial, groups, sharpness, weighted, posteriors, out):
    listed, images = posteriors.shape
    rows, _, cols = weighted.shape
    chunks = images // LANES
    half = listed // 2
    square_mask = diagonal(listed)
    lane = lax.broadcasted_iota(jnp.int32, (half, LANES), 1)
    scores = None
    power = None
    for k in range(partial.shape[0]):
        value = partial[k].astype(jnp.int32).astype(f32)
        extra = value[chunks * listed :]
        place = half + chunks
        power_code = jnp.sum(jnp.where(square_mask, extra[place : place + 1], 0.0), axis=1, keepdims=True)
        row_level = level_of(0.5 * power_code) * (1.0 / top)
        power_level = level_of(power_code) * (1.0 / top)
        image_level = [level_of(extra[half + c : half + c + 1]) for c in range(chunks)]
        part = [value[c * listed : (c + 1) * listed] * row_level * image_level[c] for c in range(chunks)]
        scores = part if scores is None else [a + b for a, b in zip(scores, part)]
        part = extra[:half] + pltpu.roll(extra[:half], LANES - 2 * group_total, 1) * (1.0 / top)
        part = part * jnp.where(lane < group_total, power_level[:half], power_level[half:])
        power = part if power is None else power + part
    scores = jnp.concatenate(scores, axis=1)
    power = jnp.where(lane < 2 * group_total, power, 0.0)
    scale = 1.0 / jnp.sqrt(power + epsilon)
    scale = jnp.concatenate([scale, pltpu.roll(scale, LANES - group_total, 1)], axis=0)
    parts = []
    for _ in range(3):
        parts.append(scale.astype(bf16))
        scale = scale - parts[-1].astype(f32)
    member = one_hot(lax.broadcasted_iota(jnp.int32, (group_total, images), 0) == groups[...])
    member = jnp.concatenate([member, jnp.zeros((LANES - group_total, images), bf16)], axis=0)
    picked = dot(jnp.concatenate(parts, axis=0), member, ((1,), (0,)))
    picked = picked[:listed] + picked[listed : 2 * listed] + picked[2 * listed :]
    logits = sharpness[...] * scores * picked
    logits = jnp.exp(logits - jnp.max(logits, axis=0, keepdims=True))
    result = logits / jnp.sum(logits, axis=0, keepdims=True)
    posteriors[...] = result
    rounded = result.astype(bf16)
    totals = [dot(rounded, weighted[r], ((1,), (0,))) for r in range(rows)]
    for h in range(cols // LANES):
        parts = [total[:, h * LANES : (h + 1) * LANES] for total in totals]
        parts = swap_blocks(parts, LANES // rows)
        for j in range(rows):
            out[h * rows + j] = parts[j].astype(bf16)


def project_body(rows, height, first_row, centre, tilt, received, arrived, out):
    bands, planes, _ = out.shape
    bins = centre.shape[0]
    pairs = arrived.shape[0] * arrived.shape[1]
    by_bin = dot(arrived[...].reshape(pairs, LANES), received[...].reshape(pairs, LANES), ((0,), (0,)))
    width = LANES // rows
    lane = lax.broadcasted_iota(jnp.int32, (bins, LANES), 1)
    empty = jnp.zeros((LANES - bins, 2 * LANES), bf16)
    parts = []
    for r in range(rows):
        deep = centre[...] + tilt[...] * reach_of(first_row[0] + r, planes, height)
        weights = []
        for h in range(2):
            where = ((lane % bands) * planes + h * (planes // 2) + lane // bands).astype(f32)
            weights.append(jnp.maximum(0.0, 1.0 - jnp.abs(where - deep)).astype(bf16))
        weight = jnp.concatenate([empty, jnp.concatenate(weights, axis=1)], axis=0)
        parts.append(dot(by_bin[r * width : (r + 1) * width].astype(bf16), weight, ((1,), (0,))))
    first = swap_blocks([part[:, :LANES] for part in parts], 1)
    second = swap_blocks([part[:, LANES:] for part in parts], 1)
    for j in range(bands):
        out[j] = jnp.concatenate([first[j], second[j]], axis=0).astype(bf16)


def final_body(arrived, out):
    bands = arrived.shape[0]
    wide = arrived[...].astype(f32)
    for zh in range(2):
        for vh in range(bands // 8):
            parts = [wide[vh * 8 + k, zh * 8 : (zh + 1) * 8, :] for k in range(8)]
            parts = swap_blocks(parts, LANES // 8)
            for zl in range(8):
                out[zh * 8 + zl, :, vh * LANES : (vh + 1) * LANES] = parts[zl]


def per_device(volume, images, bin_lists, bin_planes, bin_tilts, defocus, groups, precision):
    bands = lax.axis_size("vol")
    blocks = lax.axis_size("img")
    planes, strip, cols = volume.shape
    image_count, rows, _ = images.shape
    height = rows * bands
    bins = bin_planes.shape[0]
    listed = bin_lists.shape[1]
    group_total = defocus.shape[0]
    lane_halves = cols // LANES
    first_row = row_of(rows).reshape(1)

    piece_rows = planes + listed // 2
    half_group = blocks // 2
    sent = call(
        part_body,
        pltpu.VMEM((blocks, piece_rows, LANES), bf16),
        [VMEM, VMEM],
        VMEM,
    )(*in_hbm(bin_lists, volume))
    received = lax.all_to_all(sent, "img", 0, 0, tiled=True)
    stack = lax.all_to_all(received.reshape(bands, 2 * piece_rows, LANES), "vol", 0, 0, tiled=True)

    block = 256
    weighted, square, chosen, centre, tilt = call(
        functools.partial(weigh_body, block),
        (
            pltpu.HBM((rows, image_count, cols), bf16),
            jax.ShapeDtypeStruct((rows, 2, group_total, cols), bf16),
            jax.ShapeDtypeStruct((blocks, listed, LANES), bf16),
            jax.ShapeDtypeStruct((bins, LANES), f32),
            jax.ShapeDtypeStruct((bins, LANES), f32),
        ),
        [SMEM] * 5
        + [
            pl.BlockSpec((blocks, piece_rows, LANES), lambda i: (0, 0, 0)),
            pl.BlockSpec((block, rows, cols), lambda i: (i, 0, 0)),
        ],
        (
            pl.BlockSpec((rows, block, cols), lambda i: (0, i, 0)),
            pl.BlockSpec((rows, 2, group_total, cols), lambda i: (0, 0, 0, 0)),
            pl.BlockSpec((blocks, listed, LANES), lambda i: (0, 0, 0)),
            pl.BlockSpec((bins, LANES), lambda i: (0, 0)),
            pl.BlockSpec((bins, LANES), lambda i: (0, 0)),
        ),
        scratch=(
            pltpu.VMEM((group_total, rows, cols), f32),
            pltpu.VMEM((rows * rows, rows * rows), bf16),
            pltpu.VMEM((rows, rows, cols), bf16),
            pltpu.VMEM((2, group_total, rows, cols), bf16),
        ),
        grid=(image_count // block,),
        flops=40 * image_count * rows * cols,
        nbytes=4 * image_count * rows * cols,
    )(first_row, *in_hbm(defocus, groups, bin_planes, bin_tilts, received, images))

    img_index = lax.axis_index("img")
    own_row = first_row + img_index % half_group // lane_halves
    own_group = (img_index // half_group).reshape(1)
    pieces = call(
        functools.partial(template_body, strip, planes, height),
        jax.ShapeDtypeStruct((half_group, 2 * listed, LANES), bf16),
        [SMEM, SMEM, VMEM, VMEM, VMEM, VMEM],
        VMEM,
        flops=2**33,
        nbytes=2**25,
    )(own_row, own_group, centre, tilt, chosen, stack)
    halves = [list(range(half_group)), list(range(half_group, blocks))]
    templates = lax.all_to_all(pieces, "img", 0, 0, tiled=True, axis_index_groups=halves)

    payload_rows = listed * (image_count // LANES + 1)
    partial = call(
        score_body,
        jax.ShapeDtypeStruct((bands, payload_rows, LANES), jnp.int16),
        [VMEM, VMEM, VMEM],
        VMEM,
        scratch=(pltpu.VMEM((listed, LANES), f32),),
    )(templates, weighted, square)
    partial = lax.all_to_all(partial, "vol", 0, 0, tiled=True)

    posteriors, spread = call(
        functools.partial(posterior_body, group_total),
        (
            jax.ShapeDtypeStruct((listed, image_count), f32),
            jax.ShapeDtypeStruct((blocks, listed, LANES), bf16),
        ),
        [VMEM, VMEM, VMEM, VMEM],
        (VMEM, VMEM),
    )(partial, groups.reshape(1, image_count), precision.reshape(1, image_count), weighted)
    arrived = lax.all_to_all(spread, "img", 0, 0, tiled=True)

    projected = call(
        functools.partial(project_body, rows, height),
        jax.ShapeDtypeStruct((bands, planes, LANES), bf16),
        [SMEM, VMEM, VMEM, VMEM, VMEM],
        VMEM,
    )(first_row, centre, tilt, chosen, arrived)
    slabs = lax.all_to_all(projected, "vol", 0, 0, tiled=True)
    numerator = call(
        final_body,
        jax.ShapeDtypeStruct((planes, cols // blocks, height), f32),
        [VMEM],
        VMEM,
    )(slabs)
    return (posteriors.T, numerator.transpose(0, 2, 1))


def solution(mesh):
    placed = (
        P("vol", "img", None),
        P("img", "vol", None),
        P("img", None),
        P(),
        P(),
        P(),
        P("img"),
        P("img"),
    )
    return jax.shard_map(
        per_device,
        mesh=mesh,
        in_specs=placed,
        out_specs=(P("img", None), P("vol", None, "img")),
        check_vma=False,
    )
```

```python
import functools
import math

import jax
import jax.numpy as jnp
from jax import lax
from jax.experimental import pallas as pl
from jax.experimental.pallas import tpu as pltpu
from jax.sharding import PartitionSpec as P

phase_offset = math.asin(0.1) / math.pi
epsilon = 1e-05
bf16 = jnp.bfloat16
f32 = jnp.float32
LANES = 128
VMEM = pl.BlockSpec(memory_space=pltpu.VMEM)
SMEM = pl.BlockSpec(memory_space=pltpu.SMEM)


def call(body, out_shape, in_specs, out_specs, scratch=(), grid=(), flops=0, nbytes=0, vmem=16):
    return pl.pallas_call(
        body,
        out_shape=out_shape,
        grid=grid,
        in_specs=in_specs,
        out_specs=out_specs,
        scratch_shapes=list(scratch),
        cost_estimate=pl.CostEstimate(flops=flops, bytes_accessed=nbytes, transcendentals=0),
        compiler_params=pltpu.CompilerParams(vmem_limit_bytes=vmem * 2**20),
    )


def in_hbm(*arrays):
    return [pltpu.with_memory_space_constraint(array, pltpu.HBM) for array in arrays]


def dot(a, b, contract):
    return lax.dot_general(a, b, ((contract[0], contract[1]), ((), ())), preferred_element_type=f32)


def minus_sine_pi(turns):
    whole = jnp.floor(turns + 0.5)
    rest = turns - whole
    odd = whole - 2.0 * jnp.floor(whole * 0.5)
    x = rest * math.pi
    square = x * x
    total = -1.0 / 39916800.0
    for term in (1.0 / 362880.0, -1.0 / 5040.0, 1.0 / 120.0, -1.0 / 6.0, 1.0):
        total = total * square + term
    return total * x * (2.0 * odd - 1.0)


def swap_blocks(parts, stride):
    count = len(parts)
    lane = lax.broadcasted_iota(jnp.int32, parts[0].shape, parts[0].ndim - 1)
    bit = 1
    while bit < count:
        shift = stride * bit
        low = (lane & shift) == 0
        axis = parts[0].ndim - 1
        result = list(parts)
        for i in range(count):
            if i & bit:
                continue
            a, c = parts[i], parts[i | bit]
            result[i] = jnp.where(low, a, pltpu.roll(c, shift, axis))
            result[i | bit] = jnp.where(low, pltpu.roll(a, LANES - shift, axis), c)
        parts = result
        bit *= 2
    return parts


def row_of(rows):
    return lax.axis_index("vol") * rows


def reach_of(row, planes, height):
    return float(planes) * ((row.astype(f32) - (height - 1) * 0.5) * (2.0 / height))


def one_hot(mask):
    return mask.astype(f32).astype(bf16)


def part_body(lists, volume, out):
    planes, strip, cols = volume.shape
    listed = lists.shape[1]
    size = planes * strip
    here = lax.broadcasted_iota(jnp.int32, (size, size), 0)
    there = lax.broadcasted_iota(jnp.int32, (size, size), 1)
    mixer = one_hot((here % planes) * strip + here // planes == there)
    mixed = dot(mixer, volume[...].astype(f32).reshape(size, cols).astype(bf16), ((1,), (0,)))
    ids = jnp.concatenate([lists[...], jnp.zeros((1, LANES - listed), jnp.int32)], axis=1)
    ids = jnp.sum(jnp.where(diagonal(listed), ids, 0), axis=1, keepdims=True)
    lane = lax.broadcasted_iota(jnp.int32, (listed // 2, LANES), 1)
    half = LANES // 2
    hit = lane == jnp.where(lane < half, ids[: listed // 2], ids[listed // 2 :] + half)
    marked = hit.astype(f32)
    place = 0
    for r in range(strip):
        for h in range(cols // LANES):
            piece = mixed[r * planes : (r + 1) * planes, h * LANES : (h + 1) * LANES]
            piece = jnp.concatenate([piece, marked], axis=0).astype(bf16)
            out[place] = piece
            out[out.shape[0] // 2 + place] = piece
            place += 1


def weigh_body(block, first_row, defocus, groups, bin_planes, bin_tilts, received, images, out, square, chosen, centre, tilt, table, mixer, held, power):
    _, rows, cols = images.shape
    group_total = table.shape[0]

    @pl.when(pl.program_id(0) == 0)
    def _():
        row = (lax.broadcasted_iota(jnp.int32, (rows, cols), 0) + first_row[0]).astype(f32)
        col = lax.broadcasted_iota(jnp.int32, (rows, cols), 1).astype(f32)
        row_freq = (row - cols // 2) * (2.0 / cols)
        col_freq = (col - cols // 2) * (2.0 / cols)
        radius = 0.5 * (row_freq * row_freq + col_freq * col_freq)

        def one(g, _):
            value = minus_sine_pi(radius * defocus[g] + phase_offset)
            table[g] = value
            value = value * value
            high = value.astype(bf16)
            power[0, g] = high
            power[1, g] = (value - high.astype(f32)).astype(bf16)
            return 0

        lax.fori_loop(0, group_total, one, 0, unroll=4)
        size = mixer.shape[0]
        here = lax.broadcasted_iota(jnp.int32, (size, size), 0)
        there = lax.broadcasted_iota(jnp.int32, (size, size), 1)
        mixer[...] = one_hot((here % rows) * rows + here // rows == there)
        for part in range(2):
            for g in range(0, group_total, rows):
                mixed = dot(mixer[...], power[part, g : g + rows].reshape(rows * rows, cols), ((1,), (0,)))
                square[:, part, g : g + rows, :] = mixed.astype(bf16).reshape(rows, rows, cols)
        marked = received[...].astype(f32)[:, chosen.shape[1] :, :]
        chosen[...] = jnp.concatenate([pltpu.roll(marked, LANES // 2, 2), marked], axis=1).astype(bf16)
        for q in range(centre.shape[0]):
            centre[q : q + 1, :] = jnp.full((1, LANES), bin_planes[q].astype(f32))
            tilt[q : q + 1, :] = jnp.full((1, LANES), bin_tilts[q])

    base = pl.program_id(0) * block

    def some(k, _):
        for m in range(rows):
            n = k * rows + m
            held[m] = (images[n].astype(f32) * table[groups[base + n]]).astype(bf16)
        mixed = dot(mixer[...], held[...].reshape(rows * rows, cols), ((1,), (0,)))
        out[:, pl.ds(k * rows, rows), :] = mixed.astype(bf16).reshape(rows, rows, cols)
        return 0

    lax.fori_loop(0, block // rows, some, 0, unroll=True)


def template_body(strip, slab, height, row, group, centre, tilt, chosen, planes, out):
    bands, both, _ = planes.shape
    bins = centre.shape[0]
    peers, listed = out.shape[0], out.shape[1] // 2
    total = bands * slab
    where = lax.broadcasted_iota(jnp.int32, (bins, total), 1).astype(f32)
    picker = chosen[pl.ds(group[0] * peers, peers)].reshape(peers * listed, LANES)
    values = planes[...].astype(f32)
    empty = jnp.zeros((LANES - bins, LANES), bf16)
    for h in range(2):
        deep = centre[...] + tilt[...] * reach_of(row[0] + h * strip, slab, height)
        deep = jnp.concatenate([deep] * (total // LANES), axis=1)
        weight = jnp.maximum(0.0, 1.0 - jnp.abs(where - deep)).astype(bf16)
        start = h * (both // 2)
        rows = values[:, start : start + slab, :].reshape(total, LANES).astype(bf16)
        table = jnp.concatenate([empty, dot(weight, rows, ((1,), (0,))).astype(bf16)], axis=0)
        picked = dot(picker, table, ((1,), (0,))).astype(bf16)
        out[:, h * listed : (h + 1) * listed, :] = picked.reshape(peers, listed, LANES)


top = 32767.0


def level_code(largest):
    return jnp.floor(256.0 * jnp.log2(jnp.maximum(largest, 1e-30))) + 2.0


def level_of(code):
    return jnp.exp2(code * (1.0 / 256.0))


def diagonal(count):
    shape = (count, LANES)
    return lax.broadcasted_iota(jnp.int32, shape, 0) == lax.broadcasted_iota(jnp.int32, shape, 1)


def score_body(templates, weighted, square, out, extra):
    rows, images, cols = weighted.shape
    group_total = square.shape[0]
    listed = templates.shape[1] // 2
    total = None
    power = None
    strip = rows // 2
    for r in range(rows):
        start = r // strip * listed
        piece = [templates[2 * (r % strip) + k, start : start + listed, :] for k in range(cols // LANES)]
        piece = jnp.concatenate(piece, axis=1)
        part = dot(piece, weighted[r], ((1,), (1,)))
        total = part if total is None else total + part
        wide = piece.astype(f32)
        wide = wide * wide
        high = wide.astype(bf16)
        low = (wide - high.astype(f32)).astype(bf16)
        left = jnp.concatenate([high, high, low], axis=1)
        right = jnp.concatenate([square[r, 0], square[r, 1], square[r, 0]], axis=1)
        part = dot(left, right, ((1,), (1,)))
        power = part if power is None else power + part
    group_total = power.shape[1]
    extra[...] = jnp.zeros_like(extra)
    extra[:, :group_total] = power
    power = jnp.maximum(extra[...], 0.0)
    power_code = level_code(jnp.max(power, axis=1, keepdims=True))
    power = jnp.minimum(power * level_of(-power_code), 1.0) * top
    total = total * level_of(-0.5 * power_code)
    image_code = level_code(jnp.max(jnp.abs(total), axis=0, keepdims=True))
    total = jnp.clip(jnp.floor(total * level_of(-image_code) * top + 0.5), -top, top)
    high = jnp.floor(power)
    low = jnp.floor((power - high) * top + 0.5)
    half = listed // 2
    extra[:half] = (
        high[:half]
        + pltpu.roll(high[half:], group_total, 1)
        + pltpu.roll(low[:half], 2 * group_total, 1)
        + pltpu.roll(low[half:], 3 * group_total, 1)
    )
    chunks = images // LANES
    for c in range(chunks):
        extra[half + c : half + c + 1, :] = image_code[:, c * LANES : (c + 1) * LANES]
    square_mask = diagonal(listed)
    place = half + chunks
    extra[place : place + 1, :] = jnp.sum(jnp.where(square_mask, power_code, 0.0), axis=0, keepdims=True)
    extra[place + 1 :, :] = jnp.zeros((listed - place - 1, LANES), f32)
    pieces = [total[:, c * LANES : (c + 1) * LANES] for c in range(chunks)] + [extra[...]]
    pieces = [piece.astype(jnp.int32).astype(jnp.int16) for piece in pieces]
    for k in range(out.shape[0]):
        for c, piece in enumerate(pieces):
            out[k, c * listed : (c + 1) * listed, :] = piece


def posterior_body(group_total, partial, groups, sharpness, weighted, posteriors, out):
    listed, images = posteriors.shape
    rows, _, cols = weighted.shape
    chunks = images // LANES
    half = listed // 2
    square_mask = diagonal(listed)
    lane = lax.broadcasted_iota(jnp.int32, (half, LANES), 1)
    scores = None
    power = None
    for k in range(partial.shape[0]):
        value = partial[k].astype(jnp.int32).astype(f32)
        extra = value[chunks * listed :]
        place = half + chunks
        power_code = jnp.sum(jnp.where(square_mask, extra[place : place + 1], 0.0), axis=1, keepdims=True)
        row_level = level_of(0.5 * power_code) * (1.0 / top)
        power_level = level_of(power_code) * (1.0 / top)
        image_level = [level_of(extra[half + c : half + c + 1]) for c in range(chunks)]
        part = [value[c * listed : (c + 1) * listed] * row_level * image_level[c] for c in range(chunks)]
        scores = part if scores is None else [a + b for a, b in zip(scores, part)]
        part = extra[:half] + pltpu.roll(extra[:half], LANES - 2 * group_total, 1) * (1.0 / top)
        part = part * jnp.where(lane < group_total, power_level[:half], power_level[half:])
        power = part if power is None else power + part
    scores = jnp.concatenate(scores, axis=1)
    power = jnp.where(lane < 2 * group_total, power, 0.0)
    scale = 1.0 / jnp.sqrt(power + epsilon)
    scale = jnp.concatenate([scale, pltpu.roll(scale, LANES - group_total, 1)], axis=0)
    parts = []
    for _ in range(3):
        parts.append(scale.astype(bf16))
        scale = scale - parts[-1].astype(f32)
    member = one_hot(lax.broadcasted_iota(jnp.int32, (group_total, images), 0) == groups[...])
    member = jnp.concatenate([member, jnp.zeros((LANES - group_total, images), bf16)], axis=0)
    picked = dot(jnp.concatenate(parts, axis=0), member, ((1,), (0,)))
    picked = picked[:listed] + picked[listed : 2 * listed] + picked[2 * listed :]
    logits = sharpness[...] * scores * picked
    logits = jnp.exp(logits - jnp.max(logits, axis=0, keepdims=True))
    result = logits / jnp.sum(logits, axis=0, keepdims=True)
    posteriors[...] = result
    rounded = result.astype(bf16)
    totals = [dot(rounded, weighted[r], ((1,), (0,))) for r in range(rows)]
    for h in range(cols // LANES):
        parts = [total[:, h * LANES : (h + 1) * LANES] for total in totals]
        parts = swap_blocks(parts, LANES // rows)
        for j in range(rows):
            out[h * rows + j] = parts[j].astype(bf16)


def project_body(rows, height, first_row, centre, tilt, received, arrived, out):
    bands, planes, _ = out.shape
    bins = centre.shape[0]
    pairs = arrived.shape[0] * arrived.shape[1]
    by_bin = dot(arrived[...].reshape(pairs, LANES), received[...].reshape(pairs, LANES), ((0,), (0,)))
    width = LANES // rows
    lane = lax.broadcasted_iota(jnp.int32, (bins, LANES), 1)
    empty = jnp.zeros((LANES - bins, 2 * LANES), bf16)
    parts = []
    for r in range(rows):
        deep = centre[...] + tilt[...] * reach_of(first_row[0] + r, planes, height)
        weights = []
        for h in range(2):
            where = ((lane % bands) * planes + h * (planes // 2) + lane // bands).astype(f32)
            weights.append(jnp.maximum(0.0, 1.0 - jnp.abs(where - deep)).astype(bf16))
        weight = jnp.concatenate([empty, jnp.concatenate(weights, axis=1)], axis=0)
        parts.append(dot(by_bin[r * width : (r + 1) * width].astype(bf16), weight, ((1,), (0,))))
    first = swap_blocks([part[:, :LANES] for part in parts], 1)
    second = swap_blocks([part[:, LANES:] for part in parts], 1)
    for j in range(bands):
        out[j] = jnp.concatenate([first[j], second[j]], axis=0).astype(bf16)


def final_body(arrived, out):
    bands = arrived.shape[0]
    wide = arrived[...].astype(f32)
    for zh in range(2):
        for vh in range(bands // 8):
            parts = [wide[vh * 8 + k, zh * 8 : (zh + 1) * 8, :] for k in range(8)]
            parts = swap_blocks(parts, LANES // 8)
            for zl in range(8):
                out[zh * 8 + zl, :, vh * LANES : (vh + 1) * LANES] = parts[zl]


def per_device(volume, images, bin_lists, bin_planes, bin_tilts, defocus, groups, precision):
    bands = lax.axis_size("vol")
    blocks = lax.axis_size("img")
    planes, strip, cols = volume.shape
    image_count, rows, _ = images.shape
    height = rows * bands
    bins = bin_planes.shape[0]
    listed = bin_lists.shape[1]
    group_total = defocus.shape[0]
    lane_halves = cols // LANES
    first_row = row_of(rows).reshape(1)

    piece_rows = planes + listed // 2
    half_group = blocks // 2
    sent = call(
        part_body,
        pltpu.VMEM((blocks, piece_rows, LANES), bf16),
        [VMEM, VMEM],
        VMEM,
    )(*in_hbm(bin_lists, volume))
    received = lax.all_to_all(sent, "img", 0, 0, tiled=True)
    stack = lax.all_to_all(received[:, :planes].reshape(bands, 2 * planes, LANES), "vol", 0, 0, tiled=True)

    block = 256
    weighted, square, chosen, centre, tilt = call(
        functools.partial(weigh_body, block),
        (
            pltpu.HBM((rows, image_count, cols), bf16),
            jax.ShapeDtypeStruct((rows, 2, group_total, cols), bf16),
            jax.ShapeDtypeStruct((blocks, listed, LANES), bf16),
            jax.ShapeDtypeStruct((bins, LANES), f32),
            jax.ShapeDtypeStruct((bins, LANES), f32),
        ),
        [SMEM] * 5
        + [
            pl.BlockSpec((blocks, piece_rows, LANES), lambda i: (0, 0, 0)),
            pl.BlockSpec((block, rows, cols), lambda i: (i, 0, 0)),
        ],
        (
            pl.BlockSpec((rows, block, cols), lambda i: (0, i, 0)),
            pl.BlockSpec((rows, 2, group_total, cols), lambda i: (0, 0, 0, 0)),
            pl.BlockSpec((blocks, listed, LANES), lambda i: (0, 0, 0)),
            pl.BlockSpec((bins, LANES), lambda i: (0, 0)),
            pl.BlockSpec((bins, LANES), lambda i: (0, 0)),
        ),
        scratch=(
            pltpu.VMEM((group_total, rows, cols), f32),
            pltpu.VMEM((rows * rows, rows * rows), bf16),
            pltpu.VMEM((rows, rows, cols), bf16),
            pltpu.VMEM((2, group_total, rows, cols), bf16),
        ),
        grid=(image_count // block,),
        flops=40 * image_count * rows * cols,
        nbytes=4 * image_count * rows * cols,
    )(first_row, *in_hbm(defocus, groups, bin_planes, bin_tilts, received, images))

    img_index = lax.axis_index("img")
    own_row = first_row + img_index % half_group // lane_halves
    own_group = (img_index // half_group).reshape(1)
    pieces = call(
        functools.partial(template_body, strip, planes, height),
        jax.ShapeDtypeStruct((half_group, 2 * listed, LANES), bf16),
        [SMEM, SMEM, VMEM, VMEM, VMEM, VMEM],
        VMEM,
        flops=2**33,
        nbytes=2**25,
    )(own_row, own_group, centre, tilt, chosen, stack)
    halves = [list(range(half_group)), list(range(half_group, blocks))]
    templates = lax.all_to_all(pieces, "img", 0, 0, tiled=True, axis_index_groups=halves)

    payload_rows = listed * (image_count // LANES + 1)
    partial = call(
        score_body,
        jax.ShapeDtypeStruct((bands, payload_rows, LANES), jnp.int16),
        [VMEM, VMEM, VMEM],
        VMEM,
        scratch=(pltpu.VMEM((listed, LANES), f32),),
    )(templates, weighted, square)
    partial = lax.all_to_all(partial, "vol", 0, 0, tiled=True)

    posteriors, spread = call(
        functools.partial(posterior_body, group_total),
        (
            jax.ShapeDtypeStruct((listed, image_count), f32),
            jax.ShapeDtypeStruct((blocks, listed, LANES), bf16),
        ),
        [VMEM, VMEM, VMEM, VMEM],
        (VMEM, VMEM),
    )(partial, groups.reshape(1, image_count), precision.reshape(1, image_count), weighted)
    arrived = lax.all_to_all(spread, "img", 0, 0, tiled=True)

    projected = call(
        functools.partial(project_body, rows, height),
        jax.ShapeDtypeStruct((bands, planes, LANES), bf16),
        [SMEM, VMEM, VMEM, VMEM, VMEM],
        VMEM,
    )(first_row, centre, tilt, chosen, arrived)
    slabs = lax.all_to_all(projected, "vol", 0, 0, tiled=True)
    numerator = call(
        final_body,
        jax.ShapeDtypeStruct((planes, cols // blocks, height), f32),
        [VMEM],
        VMEM,
    )(slabs)
    return (posteriors.T, numerator.transpose(0, 2, 1))


def solution(mesh):
    placed = (
        P("vol", "img", None),
        P("img", "vol", None),
        P("img", None),
        P(),
        P(),
        P(),
        P("img"),
        P("img"),
    )
    return jax.shard_map(
        per_device,
        mesh=mesh,
        in_specs=placed,
        out_specs=(P("img", None), P("vol", None, "img")),
        check_vma=False,
    )
```

```python
import functools
import math

import jax
import jax.numpy as jnp
from jax import lax
from jax.experimental import pallas as pl
from jax.experimental.pallas import tpu as pltpu
from jax.sharding import PartitionSpec as P

phase_offset = math.asin(0.1) / math.pi
epsilon = 1e-05
bf16 = jnp.bfloat16
f32 = jnp.float32
LANES = 128
VMEM = pl.BlockSpec(memory_space=pltpu.VMEM)
SMEM = pl.BlockSpec(memory_space=pltpu.SMEM)


def call(body, out_shape, in_specs, out_specs, scratch=(), grid=(), flops=0, nbytes=0, vmem=16):
    return pl.pallas_call(
        body,
        out_shape=out_shape,
        grid=grid,
        in_specs=in_specs,
        out_specs=out_specs,
        scratch_shapes=list(scratch),
        cost_estimate=pl.CostEstimate(flops=flops, bytes_accessed=nbytes, transcendentals=0),
        compiler_params=pltpu.CompilerParams(vmem_limit_bytes=vmem * 2**20),
    )


def in_hbm(*arrays):
    return [pltpu.with_memory_space_constraint(array, pltpu.HBM) for array in arrays]


def dot(a, b, contract):
    return lax.dot_general(a, b, ((contract[0], contract[1]), ((), ())), preferred_element_type=f32)


def minus_sine_pi(turns):
    whole = jnp.floor(turns + 0.5)
    rest = turns - whole
    odd = whole - 2.0 * jnp.floor(whole * 0.5)
    x = rest * math.pi
    square = x * x
    total = -1.0 / 39916800.0
    for term in (1.0 / 362880.0, -1.0 / 5040.0, 1.0 / 120.0, -1.0 / 6.0, 1.0):
        total = total * square + term
    return total * x * (2.0 * odd - 1.0)


def swap_blocks(parts, stride):
    count = len(parts)
    lane = lax.broadcasted_iota(jnp.int32, parts[0].shape, parts[0].ndim - 1)
    bit = 1
    while bit < count:
        shift = stride * bit
        low = (lane & shift) == 0
        axis = parts[0].ndim - 1
        result = list(parts)
        for i in range(count):
            if i & bit:
                continue
            a, c = parts[i], parts[i | bit]
            result[i] = jnp.where(low, a, pltpu.roll(c, shift, axis))
            result[i | bit] = jnp.where(low, pltpu.roll(a, LANES - shift, axis), c)
        parts = result
        bit *= 2
    return parts


def row_of(rows):
    return lax.axis_index("vol") * rows


def reach_of(row, planes, height):
    return float(planes) * ((row.astype(f32) - (height - 1) * 0.5) * (2.0 / height))


def one_hot(mask):
    return mask.astype(f32).astype(bf16)


def part_body(lists, volume, out):
    planes, strip, cols = volume.shape
    listed = lists.shape[1]
    size = planes * strip
    here = lax.broadcasted_iota(jnp.int32, (size, size), 0)
    there = lax.broadcasted_iota(jnp.int32, (size, size), 1)
    mixer = one_hot((here % planes) * strip + here // planes == there)
    mixed = dot(mixer, volume[...].astype(f32).reshape(size, cols).astype(bf16), ((1,), (0,)))
    ids = jnp.concatenate([lists[...], jnp.zeros((1, LANES - listed), jnp.int32)], axis=1)
    ids = jnp.sum(jnp.where(diagonal(listed), ids, 0), axis=1, keepdims=True)
    lane = lax.broadcasted_iota(jnp.int32, (listed // 2, LANES), 1)
    half = LANES // 2
    hit = lane == jnp.where(lane < half, ids[: listed // 2], ids[listed // 2 :] + half)
    marked = hit.astype(f32)
    place = 0
    for r in range(strip):
        for h in range(cols // LANES):
            piece = mixed[r * planes : (r + 1) * planes, h * LANES : (h + 1) * LANES]
            piece = jnp.concatenate([piece, marked], axis=0).astype(bf16)
            out[place] = piece
            out[out.shape[0] // 2 + place] = piece
            place += 1


def weigh_body(block, first_row, defocus, groups, bin_planes, bin_tilts, received, images, out, square, chosen, centre, tilt, table, mixer, held, power):
    _, rows, cols = images.shape
    group_total = table.shape[0]

    @pl.when(pl.program_id(0) == 0)
    def _():
        row = (lax.broadcasted_iota(jnp.int32, (rows, cols), 0) + first_row[0]).astype(f32)
        col = lax.broadcasted_iota(jnp.int32, (rows, cols), 1).astype(f32)
        row_freq = (row - cols // 2) * (2.0 / cols)
        col_freq = (col - cols // 2) * (2.0 / cols)
        radius = 0.5 * (row_freq * row_freq + col_freq * col_freq)

        def one(g, _):
            value = minus_sine_pi(radius * defocus[g] + phase_offset)
            table[g] = value
            value = value * value
            high = value.astype(bf16)
            power[0, g] = high
            power[1, g] = (value - high.astype(f32)).astype(bf16)
            return 0

        lax.fori_loop(0, group_total, one, 0, unroll=4)
        size = mixer.shape[0]
        here = lax.broadcasted_iota(jnp.int32, (size, size), 0)
        there = lax.broadcasted_iota(jnp.int32, (size, size), 1)
        mixer[...] = one_hot((here % rows) * rows + here // rows == there)
        for part in range(2):
            for g in range(0, group_total, rows):
                mixed = dot(mixer[...], power[part, g : g + rows].reshape(rows * rows, cols), ((1,), (0,)))
                square[:, part, g : g + rows, :] = mixed.astype(bf16).reshape(rows, rows, cols)
        marked = received[...].astype(f32)[:, chosen.shape[1] :, :]
        chosen[...] = jnp.concatenate([pltpu.roll(marked, LANES // 2, 2), marked], axis=1).astype(bf16)
        for q in range(centre.shape[0]):
            centre[q : q + 1, :] = jnp.full((1, LANES), bin_planes[q].astype(f32))
            tilt[q : q + 1, :] = jnp.full((1, LANES), bin_tilts[q])

    base = pl.program_id(0) * block

    def some(k, _):
        for m in range(rows):
            n = k * rows + m
            held[m] = (images[n].astype(f32) * table[groups[base + n]]).astype(bf16)
        mixed = dot(mixer[...], held[...].reshape(rows * rows, cols), ((1,), (0,)))
        out[:, pl.ds(k * rows, rows), :] = mixed.astype(bf16).reshape(rows, rows, cols)
        return 0

    lax.fori_loop(0, block // rows, some, 0, unroll=True)


def template_body(strip, slab, height, row, group, centre, tilt, chosen, planes, out):
    bands, both, _ = planes.shape
    bins = centre.shape[0]
    peers, listed = out.shape[0], out.shape[1] // 2
    total = bands * slab
    where = lax.broadcasted_iota(jnp.int32, (bins, total), 1).astype(f32)
    picker = chosen[pl.ds(group[0] * peers, peers)].reshape(peers * listed, LANES)
    values = planes[...].astype(f32)
    empty = jnp.zeros((LANES - bins, LANES), bf16)
    for h in range(2):
        deep = centre[...] + tilt[...] * reach_of(row[0] + h * strip, slab, height)
        deep = jnp.concatenate([deep] * (total // LANES), axis=1)
        weight = jnp.maximum(0.0, 1.0 - jnp.abs(where - deep)).astype(bf16)
        start = h * (both // 2)
        rows = values[:, start : start + slab, :].reshape(total, LANES).astype(bf16)
        table = jnp.concatenate([empty, dot(weight, rows, ((1,), (0,))).astype(bf16)], axis=0)
        picked = dot(picker, table, ((1,), (0,))).astype(bf16)
        out[:, h * listed : (h + 1) * listed, :] = picked.reshape(peers, listed, LANES)


top = 32767.0


def level_code(largest):
    return jnp.floor(256.0 * jnp.log2(jnp.maximum(largest, 1e-30))) + 2.0


def level_of(code):
    return jnp.exp2(code * (1.0 / 256.0))


def diagonal(count):
    shape = (count, LANES)
    return lax.broadcasted_iota(jnp.int32, shape, 0) == lax.broadcasted_iota(jnp.int32, shape, 1)


def score_body(templates, weighted, square, out, extra):
    rows, images, cols = weighted.shape
    group_total = square.shape[0]
    listed = templates.shape[1] // 2
    total = None
    power = None
    strip = rows // 2
    for r in range(rows):
        start = r // strip * listed
        piece = [templates[2 * (r % strip) + k, start : start + listed, :] for k in range(cols // LANES)]
        piece = jnp.concatenate(piece, axis=1)
        part = dot(piece, weighted[r], ((1,), (1,)))
        total = part if total is None else total + part
        wide = piece.astype(f32)
        wide = wide * wide
        high = wide.astype(bf16)
        low = (wide - high.astype(f32)).astype(bf16)
        left = jnp.concatenate([high, high, low], axis=1)
        right = jnp.concatenate([square[r, 0], square[r, 1], square[r, 0]], axis=1)
        part = dot(left, right, ((1,), (1,)))
        power = part if power is None else power + part
    group_total = power.shape[1]
    extra[...] = jnp.zeros_like(extra)
    extra[:, :group_total] = power
    power = jnp.maximum(extra[...], 0.0)
    power_code = level_code(jnp.max(power, axis=1, keepdims=True))
    power = jnp.minimum(power * level_of(-power_code), 1.0) * top
    total = total * level_of(-0.5 * power_code)
    image_code = level_code(jnp.max(jnp.abs(total), axis=0, keepdims=True))
    total = jnp.clip(jnp.floor(total * level_of(-image_code) * top + 0.5), -top, top)
    high = jnp.floor(power)
    low = jnp.floor((power - high) * top + 0.5)
    half = listed // 2
    extra[:half] = (
        high[:half]
        + pltpu.roll(high[half:], group_total, 1)
        + pltpu.roll(low[:half], 2 * group_total, 1)
        + pltpu.roll(low[half:], 3 * group_total, 1)
    )
    chunks = images // LANES
    for c in range(chunks):
        extra[half + c : half + c + 1, :] = image_code[:, c * LANES : (c + 1) * LANES]
    square_mask = diagonal(listed)
    place = half + chunks
    extra[place : place + 1, :] = jnp.sum(jnp.where(square_mask, power_code, 0.0), axis=0, keepdims=True)
    extra[place + 1 :, :] = jnp.zeros((listed - place - 1, LANES), f32)
    pieces = [total[:, c * LANES : (c + 1) * LANES] for c in range(chunks)] + [extra[...]]
    pieces = [piece.astype(jnp.int32).astype(jnp.int16) for piece in pieces]
    for k in range(out.shape[0]):
        for c, piece in enumerate(pieces):
            out[k, c * listed : (c + 1) * listed, :] = piece


def posterior_body(group_total, partial, groups, sharpness, weighted, posteriors, out):
    listed, images = posteriors.shape
    rows, _, cols = weighted.shape
    chunks = images // LANES
    half = listed // 2
    square_mask = diagonal(listed)
    lane = lax.broadcasted_iota(jnp.int32, (half, LANES), 1)
    scores = None
    power = None
    for k in range(partial.shape[0]):
        value = partial[k].astype(jnp.int32).astype(f32)
        extra = value[chunks * listed :]
        place = half + chunks
        power_code = jnp.sum(jnp.where(square_mask, extra[place : place + 1], 0.0), axis=1, keepdims=True)
        row_level = level_of(0.5 * power_code)
        power_level = row_level * row_level * (1.0 / top)
        row_level = row_level * (1.0 / top)
        image_level = [level_of(extra[half + c : half + c + 1]) for c in range(chunks)]
        part = [value[c * listed : (c + 1) * listed] * row_level * image_level[c] for c in range(chunks)]
        scores = part if scores is None else [a + b for a, b in zip(scores, part)]
        part = extra[:half] + pltpu.roll(extra[:half], LANES - 2 * group_total, 1) * (1.0 / top)
        part = part * jnp.where(lane < group_total, power_level[:half], power_level[half:])
        power = part if power is None else power + part
    scores = jnp.concatenate(scores, axis=1)
    power = jnp.where(lane < 2 * group_total, power, 0.0)
    scale = 1.0 / jnp.sqrt(power + epsilon)
    scale = jnp.concatenate([scale, pltpu.roll(scale, LANES - group_total, 1)], axis=0)
    parts = []
    for _ in range(3):
        parts.append(scale.astype(bf16))
        scale = scale - parts[-1].astype(f32)
    member = one_hot(lax.broadcasted_iota(jnp.int32, (group_total, images), 0) == groups[...])
    member = jnp.concatenate([member, jnp.zeros((LANES - group_total, images), bf16)], axis=0)
    picked = dot(jnp.concatenate(parts, axis=0), member, ((1,), (0,)))
    picked = picked[:listed] + picked[listed : 2 * listed] + picked[2 * listed :]
    logits = sharpness[...] * scores * picked
    logits = jnp.exp(logits - jnp.max(logits, axis=0, keepdims=True))
    result = logits / jnp.sum(logits, axis=0, keepdims=True)
    posteriors[...] = result
    rounded = result.astype(bf16)
    totals = [dot(rounded, weighted[r], ((1,), (0,))) for r in range(rows)]
    for h in range(cols // LANES):
        parts = [total[:, h * LANES : (h + 1) * LANES] for total in totals]
        parts = swap_blocks(parts, LANES // rows)
        for j in range(rows):
            out[h * rows + j] = parts[j].astype(bf16)


def project_body(rows, height, first_row, centre, tilt, received, arrived, out):
    bands, planes, _ = out.shape
    bins = centre.shape[0]
    pairs = arrived.shape[0] * arrived.shape[1]
    by_bin = dot(arrived[...].reshape(pairs, LANES), received[...].reshape(pairs, LANES), ((0,), (0,)))
    width = LANES // rows
    lane = lax.broadcasted_iota(jnp.int32, (bins, LANES), 1)
    empty = jnp.zeros((LANES - bins, 2 * LANES), bf16)
    parts = []
    for r in range(rows):
        deep = centre[...] + tilt[...] * reach_of(first_row[0] + r, planes, height)
        weights = []
        for h in range(2):
            where = ((lane % bands) * planes + h * (planes // 2) + lane // bands).astype(f32)
            weights.append(jnp.maximum(0.0, 1.0 - jnp.abs(where - deep)).astype(bf16))
        weight = jnp.concatenate([empty, jnp.concatenate(weights, axis=1)], axis=0)
        parts.append(dot(by_bin[r * width : (r + 1) * width].astype(bf16), weight, ((1,), (0,))))
    first = swap_blocks([part[:, :LANES] for part in parts], 1)
    second = swap_blocks([part[:, LANES:] for part in parts], 1)
    for j in range(bands):
        out[j] = jnp.concatenate([first[j], second[j]], axis=0).astype(bf16)


def final_body(arrived, out):
    bands = arrived.shape[0]
    wide = arrived[...].astype(f32)
    for zh in range(2):
        for vh in range(bands // 8):
            parts = [wide[vh * 8 + k, zh * 8 : (zh + 1) * 8, :] for k in range(8)]
            parts = swap_blocks(parts, LANES // 8)
            for zl in range(8):
                out[zh * 8 + zl, :, vh * LANES : (vh + 1) * LANES] = parts[zl]


def per_device(volume, images, bin_lists, bin_planes, bin_tilts, defocus, groups, precision):
    bands = lax.axis_size("vol")
    blocks = lax.axis_size("img")
    planes, strip, cols = volume.shape
    image_count, rows, _ = images.shape
    height = rows * bands
    bins = bin_planes.shape[0]
    listed = bin_lists.shape[1]
    group_total = defocus.shape[0]
    lane_halves = cols // LANES
    first_row = row_of(rows).reshape(1)

    piece_rows = planes + listed // 2
    half_group = blocks // 2
    sent = call(
        part_body,
        pltpu.VMEM((blocks, piece_rows, LANES), bf16),
        [VMEM, VMEM],
        VMEM,
    )(*in_hbm(bin_lists, volume))
    received = lax.all_to_all(sent, "img", 0, 0, tiled=True)
    stack = lax.all_to_all(received.reshape(bands, 2 * piece_rows, LANES), "vol", 0, 0, tiled=True)

    block = 256
    weighted, square, chosen, centre, tilt = call(
        functools.partial(weigh_body, block),
        (
            pltpu.HBM((rows, image_count, cols), bf16),
            jax.ShapeDtypeStruct((rows, 2, group_total, cols), bf16),
            jax.ShapeDtypeStruct((blocks, listed, LANES), bf16),
            jax.ShapeDtypeStruct((bins, LANES), f32),
            jax.ShapeDtypeStruct((bins, LANES), f32),
        ),
        [SMEM] * 5
        + [
            pl.BlockSpec((blocks, piece_rows, LANES), lambda i: (0, 0, 0)),
            pl.BlockSpec((block, rows, cols), lambda i: (i, 0, 0)),
        ],
        (
            pl.BlockSpec((rows, block, cols), lambda i: (0, i, 0)),
            pl.BlockSpec((rows, 2, group_total, cols), lambda i: (0, 0, 0, 0)),
            pl.BlockSpec((blocks, listed, LANES), lambda i: (0, 0, 0)),
            pl.BlockSpec((bins, LANES), lambda i: (0, 0)),
            pl.BlockSpec((bins, LANES), lambda i: (0, 0)),
        ),
        scratch=(
            pltpu.VMEM((group_total, rows, cols), f32),
            pltpu.VMEM((rows * rows, rows * rows), bf16),
            pltpu.VMEM((rows, rows, cols), bf16),
            pltpu.VMEM((2, group_total, rows, cols), bf16),
        ),
        grid=(image_count // block,),
        flops=40 * image_count * rows * cols,
        nbytes=4 * image_count * rows * cols,
    )(first_row, *in_hbm(defocus, groups, bin_planes, bin_tilts, received, images))

    img_index = lax.axis_index("img")
    own_row = first_row + img_index % half_group // lane_halves
    own_group = (img_index // half_group).reshape(1)
    pieces = call(
        functools.partial(template_body, strip, planes, height),
        jax.ShapeDtypeStruct((half_group, 2 * listed, LANES), bf16),
        [SMEM, SMEM, VMEM, VMEM, VMEM, VMEM],
        VMEM,
        flops=2**33,
        nbytes=2**25,
    )(own_row, own_group, centre, tilt, chosen, stack)
    halves = [list(range(half_group)), list(range(half_group, blocks))]
    templates = lax.all_to_all(pieces, "img", 0, 0, tiled=True, axis_index_groups=halves)

    payload_rows = listed * (image_count // LANES + 1)
    partial = call(
        score_body,
        jax.ShapeDtypeStruct((bands, payload_rows, LANES), jnp.int16),
        [VMEM, VMEM, VMEM],
        VMEM,
        scratch=(pltpu.VMEM((listed, LANES), f32),),
    )(templates, weighted, square)
    partial = lax.all_to_all(partial, "vol", 0, 0, tiled=True)

    posteriors, spread = call(
        functools.partial(posterior_body, group_total),
        (
            jax.ShapeDtypeStruct((listed, image_count), f32),
            jax.ShapeDtypeStruct((blocks, listed, LANES), bf16),
        ),
        [VMEM, VMEM, VMEM, VMEM],
        (VMEM, VMEM),
    )(partial, groups.reshape(1, image_count), precision.reshape(1, image_count), weighted)
    arrived = lax.all_to_all(spread, "img", 0, 0, tiled=True)

    projected = call(
        functools.partial(project_body, rows, height),
        jax.ShapeDtypeStruct((bands, planes, LANES), bf16),
        [SMEM, VMEM, VMEM, VMEM, VMEM],
        VMEM,
    )(first_row, centre, tilt, chosen, arrived)
    slabs = lax.all_to_all(projected, "vol", 0, 0, tiled=True)
    numerator = call(
        final_body,
        jax.ShapeDtypeStruct((planes, cols // blocks, height), f32),
        [VMEM],
        VMEM,
    )(slabs)
    return (posteriors.T, numerator.transpose(0, 2, 1))


def solution(mesh):
    placed = (
        P("vol", "img", None),
        P("img", "vol", None),
        P("img", None),
        P(),
        P(),
        P(),
        P("img"),
        P("img"),
    )
    return jax.shard_map(
        per_device,
        mesh=mesh,
        in_specs=placed,
        out_specs=(P("img", None), P("vol", None, "img")),
        check_vma=False,
    )
```
